128 devices in a mesh: section: 2 (over core), expert: 16 (over y, z), tensor: 4 (over x).
Axes of the slice: x: 4, y: 4, z: 4, core: 2. Of those that a mesh axis runs over, the one named last changes fastest.
Arguments:
- saved_inputs: bfloat16 [2, 8192, 2560], P('section', ('expert', 'tensor')), may hold values from -6 to 6
- out_cotangent: bfloat16 [2, 8192, 2560], P('section', ('expert', 'tensor')), may hold values from -1.5 to 1.5
- router: bfloat16 [2, 2560, 16], P('section'), may hold values from -0.125 to 0.125
- w_gate: bfloat16 [2, 16, 2560, 1536], P('section', 'expert', None, 'tensor'), may hold values from -0.125 to 0.125
- w_up: bfloat16 [2, 16, 2560, 1536], P('section', 'expert', None, 'tensor'), may hold values from -0.125 to 0.125
- w_down: bfloat16 [2, 16, 1536, 2560], P('section', 'expert', 'tensor'), may hold values from -0.15625 to 0.15625
- expert_ids: int32 [2, 8192, 2], P('section', ('expert', 'tensor')), may hold values from 0 to 15, all different within a row; in each aligned block of 128 rows (0 to 127, 128 to 255, ..., all dimensions but the last counted through in order) at most 18 rows name the same one
Outputs:
- passed_cotangent: bfloat16 [2, 8192, 2560], P('section', ('expert', 'tensor'))
- router_grad: float32 [2, 2560, 16], P('section')
- gate_grad: bfloat16 [2, 16, 2560, 1536], P('section', 'expert', None, 'tensor')
- up_grad: bfloat16 [2, 16, 2560, 1536], P('section', 'expert', None, 'tensor')
- down_grad: bfloat16 [2, 16, 1536, 2560], P('section', 'expert', 'tensor')
The draws below stay inside these ranges and needn't reach their ends.
Inputs may be any that keep to these rules, and one draw needn't show every extreme that they name: `expert_ids`: each token names 2 different experts. Among the 128 tokens of one device of one section (aligned blocks of the token dimension) no expert is named more than 18 times, and in some blocks one is named exactly 18 times.
All inputs are finite; a program needn't handle non-finite values.
Results may differ from the reference program's by a relative error of at most 0.018.
Values may be sent and summed in bfloat16 or wider, within the bound.
No kernel may reach another device: no remote copies, remote signals or barrier semaphores. Data moves between devices by JAX's collectives and lax.ppermute only.
A program may use at most 128 MiB of HBM per device.

```python
import math
import jax
import jax.numpy as jnp
import numpy as np
from jax import lax

D = 2560
FF = 1536
TOPK = 2
TOK_DEV = 128
EXPERTS = 16
TOKENS = 8192
CAP = 18
N_SECTION = 2
N_EXPERT = 16
N_TENSOR = 4


def levels(key, extent, cuts, smallest, top_value):
    factor_of, own = 1.0, jax.random.fold_in(key, 6)
    for position, blocks in cuts:
        steps = jnp.exp(jax.random.uniform(jax.random.fold_in(own, position), (blocks,), jnp.float32, smallest / len(cuts), top_value / len(cuts)))
        factor_of = factor_of * jnp.repeat(steps, extent[position] // blocks).reshape([-1 if axis == position else 1 for axis in range(len(extent))])
    return factor_of


def shared_out(own_key, own, number, rows, number_of, top, limit, slope):
    order = jax.random.permutation(own_key, number_of)
    crowded, usual = shares(number_of, rows * top, limit, slope, True), shares(number_of, rows * top, limit, slope, False)
    places = jnp.arange(number_of)

    def named(tallies, turn):
        used = int((tallies > 0).sum())
        fixed = max(1, used // 4)
        moved = fixed + (places - fixed + turn * (used - fixed)) % max(1, number_of - fixed)
        return jnp.zeros((number_of,), jnp.int32).at[order[jnp.where(places < fixed, places, moved)]].set(jnp.asarray(tallies, jnp.int32))

    tallies = jnp.where(number % 4 == 0, named(crowded, number // 4), named(usual, number - number // 4 - 1))
    mixed = jax.random.permutation(jax.random.fold_in(own, 3), number_of)
    donor, sink = mixed[0:number_of // 2 * 2:2], mixed[1:number_of // 2 * 2:2]
    slack = jnp.minimum(tallies[donor] - 1, limit - tallies[sink]) // 2
    slack = jnp.where((donor == order[0]) | (sink == order[0]) | (tallies[sink] == 0), 0, jnp.maximum(slack, 0))
    moved = jax.random.randint(jax.random.fold_in(own, 4), (number_of // 2,), 0, 1 << 20) % (slack + 1)
    tallies = tallies.at[donor].add(-moved).at[sink].add(moved)
    labels = jnp.searchsorted(jnp.cumsum(tallies), jnp.arange(rows * top), side="right").astype(jnp.int32)
    grid = labels.reshape(top, rows).T
    grid = grid[jax.random.permutation(jax.random.fold_in(own, 1), rows)]
    turn = jax.random.randint(jax.random.fold_in(own, 2), (rows, 1), 0, top)
    return jnp.take_along_axis(grid, (jnp.arange(top)[None, :] + turn) % top, axis=1)


def shares(amount, total, reach, lean, full):
    loads = [(1 << 20) // math.isqrt(rank ** lean) + 1 for rank in range(1, amount + 1)]
    largest = reach if full else min(reach, max(-(-total // amount), total * loads[0] // sum(loads)))
    least = 1 if total - largest >= amount - 1 else 0
    counts, rest = [largest] + [least] * (amount - 1), total - largest - least * (amount - 1)
    while rest > 0:
        movable = [i for i in range(1, amount) if counts[i] < largest] or [i for i in range(1, amount) if counts[i] < reach]
        whole, budget = sum([loads[i] for i in movable]), rest
        for i in movable:
            more = min(reach - counts[i], max(1, budget * loads[i] // whole), rest)
            counts[i] = counts[i] + more
            rest = rest - more
    return np.array(counts)


def bell_draw(stream_key, dims, width, limit, shards=(), kind=jnp.bfloat16):
    array = width * jax.random.normal(stream_key, dims, jnp.float32)
    if shards:
        array = array * levels(stream_key, dims, shards, -0.22, 0.18)
    return jnp.clip(array, -limit, limit).astype(kind)


def setup_inputs(seed: int = 0) -> dict:
    keys = jax.random.split(jax.random.key(seed), 8)
    saved_inputs = bell_draw(keys[0], (N_SECTION, TOKENS, D), 1.0, 6.0, ((0, 2), (1, 64)))
    out_cotangent = bell_draw(keys[1], (N_SECTION, TOKENS, D), 0.25, 1.5, ((0, 2), (1, 64)))
    router = bell_draw(keys[2], (N_SECTION, D, EXPERTS), D ** -0.5, 0.125, ((0, 2),))
    w_gate = bell_draw(keys[3], (N_SECTION, EXPERTS, D, FF), D ** -0.5, 0.125, ((0, 2), (1, 16), (3, 4)))
    w_up = bell_draw(keys[4], (N_SECTION, EXPERTS, D, FF), D ** -0.5, 0.125, ((0, 2), (1, 16), (3, 4)))
    w_down = bell_draw(keys[5], (N_SECTION, EXPERTS, FF, D), FF ** -0.5, 0.15625, ((0, 2), (1, 16), (2, 4)))
    expert_ids_keys = jax.random.split(jax.random.fold_in(keys[6], 1), N_SECTION * TOKENS // TOK_DEV)
    expert_ids_turns = jax.random.permutation(jax.random.fold_in(keys[6], 3), N_SECTION * TOKENS // TOK_DEV)
    expert_ids = jax.vmap(lambda own, number: shared_out(jax.random.fold_in(keys[6], 2), own, number, TOK_DEV, EXPERTS, TOPK, CAP, 2))(expert_ids_keys, expert_ids_turns).reshape((N_SECTION, TOKENS, TOPK))
    return dict(saved_inputs=saved_inputs, out_cotangent=out_cotangent, router=router, w_gate=w_gate, w_up=w_up, w_down=w_down, expert_ids=expert_ids)


routed_scale = 16.0


def quarter_total(values):
    rounded = lax.optimization_barrier(values.astype(jnp.bfloat16))
    return jnp.sum(rounded.astype(jnp.float32), axis=1)


def section_backward(inputs, cotang, router_w, gate_all, up_all, down_all, routes):
    logits = jnp.dot(inputs, router_w, preferred_element_type=jnp.float32)
    exp_logit = jnp.exp(logits)
    prob_rows = exp_logit / jnp.sum(exp_logit, axis=-1, keepdims=True)
    expert_iota = jnp.arange(EXPERTS, dtype=jnp.int32)
    choose = (routes[:, :, None] == expert_iota[None, None, :]).astype(jnp.float32)
    gate_vals = jnp.sum(choose * prob_rows[:, None, :], axis=2).astype(jnp.bfloat16)
    flat_ids = routes.reshape(-1)
    flat_gates = gate_vals.reshape(-1)
    row_bound = N_EXPERT * N_TENSOR * CAP
    quarter = FF // N_TENSOR

    def one_expert(running, expert):
        accumulated, pair_grad = running
        match = flat_ids == expert
        row_count = jnp.sum(match.astype(jnp.int32))
        picked = jnp.nonzero(match, size=row_bound, fill_value=0)[0].astype(jnp.int32)
        live_rows = jnp.arange(row_bound, dtype=jnp.int32) < row_count
        token_idx = picked // TOPK
        rows_in = jnp.where(live_rows[:, None], inputs[token_idx], jnp.zeros((), jnp.bfloat16))
        rows_cot = jnp.where(live_rows[:, None], cotang[token_idx], jnp.zeros((), jnp.bfloat16))
        row_gate = jnp.where(live_rows, flat_gates[picked], jnp.zeros((), jnp.bfloat16))
        gate_mat = gate_all[expert]
        up_mat = up_all[expert]
        down_mat = down_all[expert]
        hidden = jnp.dot(rows_in, gate_mat, preferred_element_type=jnp.float32)
        up_value = jnp.dot(rows_in, up_mat, preferred_element_type=jnp.float32)
        sigmoid_h = jax.nn.sigmoid(hidden)
        silu_val = hidden * sigmoid_h
        silu_slope = sigmoid_h * (1.0 + hidden * (1.0 - sigmoid_h))
        product = silu_val * up_value
        back_proj = jnp.dot(rows_cot, down_mat.T, preferred_element_type=jnp.float32)
        gate_part = jnp.sum((product * back_proj).reshape(row_bound, N_TENSOR, quarter), axis=2)
        dgate = (routed_scale * quarter_total(gate_part)).astype(jnp.bfloat16)
        scaled = routed_scale * row_gate.astype(jnp.float32)
        grad_act = scaled[:, None] * back_proj
        d_hidden = (grad_act * up_value * silu_slope).astype(jnp.bfloat16)
        d_up = (grad_act * silu_val).astype(jnp.bfloat16)
        g_act = (scaled[:, None] * product).astype(jnp.bfloat16)
        grad_down = jnp.dot(g_act.T, rows_cot, preferred_element_type=jnp.float32).astype(jnp.bfloat16)
        grad_gate = jnp.dot(rows_in.T, d_hidden, preferred_element_type=jnp.float32).astype(jnp.bfloat16)
        grad_up = jnp.dot(rows_in.T, d_up, preferred_element_type=jnp.float32).astype(jnp.bfloat16)
        hidden_q = d_hidden.astype(jnp.float32).reshape(row_bound, N_TENSOR, quarter)
        up_q = d_up.astype(jnp.float32).reshape(row_bound, N_TENSOR, quarter)
        gate_q = gate_mat.astype(jnp.float32).reshape(D, N_TENSOR, quarter)
        upmat_q = up_mat.astype(jnp.float32).reshape(D, N_TENSOR, quarter)
        partial_value = jnp.einsum("rqf,dqf->rqd", hidden_q, gate_q) + jnp.einsum("rqf,dqf->rqd", up_q, upmat_q)
        expert_cot = quarter_total(partial_value).astype(jnp.bfloat16)
        accumulated = accumulated.at[token_idx].add(
            jnp.where(live_rows[:, None], expert_cot.astype(jnp.float32), jnp.zeros((), jnp.float32)))
        pair_grad = pair_grad.at[picked].add(
            jnp.where(live_rows, dgate.astype(jnp.float32), jnp.zeros((), jnp.float32)))
        return (accumulated, pair_grad), (grad_gate, grad_up, grad_down)

    start = (jnp.zeros((TOKENS, D), jnp.float32), jnp.zeros((TOKENS * TOPK,), jnp.float32))
    (accumulated, pair_grad), (grad_gate, grad_up, grad_down) = lax.scan(one_expert, start, expert_iota)
    dprob = jnp.sum(choose * pair_grad.reshape(TOKENS, TOPK)[:, :, None], axis=1)
    dlogit = (prob_rows * (dprob - jnp.sum(prob_rows * dprob, axis=1, keepdims=True))).astype(jnp.bfloat16)
    total = cotang.astype(jnp.float32) + accumulated + jnp.dot(dlogit, router_w.T, preferred_element_type=jnp.float32)
    router_total = jnp.dot(inputs.T, dlogit, preferred_element_type=jnp.float32)
    return total.astype(jnp.bfloat16), router_total, grad_gate, grad_up, grad_down


def reference(saved_inputs, out_cotangent, router, w_gate, w_up, w_down, expert_ids):
    results = []
    for section_idx in range(N_SECTION):
        results.append(section_backward(saved_inputs[section_idx], out_cotangent[section_idx], router[section_idx],
                                      w_gate[section_idx], w_up[section_idx], w_down[section_idx], expert_ids[section_idx]))
    passed = jnp.stack([results[(section_idx + 1) % N_SECTION][0] for section_idx in range(N_SECTION)])
    router_grad = jnp.stack([item[1] for item in results])
    gate_grad = jnp.stack([item[2] for item in results])
    up_grad = jnp.stack([item[3] for item in results])
    down_grad = jnp.stack([item[4] for item in results])
    return passed, router_grad, gate_grad, up_grad, down_grad
```

```python
import jax
import jax.numpy as jnp
from jax import lax
from jax.sharding import PartitionSpec as P

routed_scale = 16.0
MAIN = 16
G_SLOT_COLS = 640
P_SLOT_COLS = 1280
bf16 = jnp.bfloat16
f32 = jnp.float32


def along_x(block, step):
    n = lax.axis_size("tensor")
    return lax.ppermute(block, "tensor", [(i, (i + step) % n) for i in range(n)])


def along_plane(block, step_y, step_z):
    n = lax.axis_size("expert")
    side = int(round(n**0.5))
    route = [
        (y * side + z, (y + step_y) % side * side + (z + step_z) % side)
        for y in range(side)
        for z in range(side)
    ]
    return lax.ppermute(block, "expert", route)


def gathered_x(block):
    half = block.shape[0] // 2
    above = along_x(block, -1)
    below = along_x(block, 1)
    far = jnp.concatenate([along_x(above[:half], -1), along_x(below[half:], 1)])
    return [block, above, far, below]


def add(a, b):
    return (a.astype(f32) + b.astype(f32)).astype(bf16)


def scattered_x(parts):
    own, up, far, down = parts
    half = own.shape[0] // 2
    from_below = along_x(far[:half], 1)
    from_above = along_x(far[half:], -1)
    up = jnp.concatenate([add(up[:half], from_below), up[half:]])
    down = jnp.concatenate([down[:half], add(down[half:], from_above)])
    return own.astype(f32) + along_x(up, 1).astype(f32) + along_x(down, -1).astype(f32)


def summed(block):
    for shift in (
        along_x,
        lambda b, d: along_plane(b, d, 0),
        lambda b, d: along_plane(b, 0, d),
    ):
        block = block + shift(block, 1) + shift(block, 2) + shift(block, 3)
    return block


def exchanged(block):
    return lax.all_to_all(block, "expert", split_axis=0, concat_axis=0, tiled=True)


def dot(a, b, contract=((1,), (0,))):
    return lax.dot_general(a, b, (contract, ((), ())), preferred_element_type=f32)


def on_device(saved_inputs, out_cotangent, router, w_gate, w_up, w_down, expert_ids):
    inputs, cotang, router_w = saved_inputs[0], out_cotangent[0], router[0]
    gate_w, up_w, down_w = w_gate[0, 0], w_up[0, 0], w_down[0, 0]
    routes = expert_ids[0]
    n_owner = lax.axis_size("expert")
    n_group = lax.axis_size("tensor")
    experts = n_owner
    tok, top = routes.shape
    width = inputs.shape[1]
    capacity = min(tok, max(2, (9 * tok * top + 8 * experts - 1) // (8 * experts)))
    extra = capacity - MAIN
    pieces = 4
    ovf = pieces * extra
    chunk = n_group * capacity
    flat_ids = routes.reshape(-1)
    flat_hot = (flat_ids[:, None] == jnp.arange(experts, dtype=jnp.int32)[None, :]).astype(f32)
    place = jnp.sum((jnp.cumsum(flat_hot, axis=0) - flat_hot) * flat_hot, axis=1)
    code = (flat_ids * 32 + place.astype(jnp.int32)).reshape(tok, top).T
    codes = [code, along_x(code, -1), along_x(code, 2), along_x(code, 1)]

    def hot(rows, n_rows):
        grid = jnp.arange(n_rows, dtype=jnp.int32)[:, None]
        return jnp.any(rows[:, None, :] == grid[None], axis=0).astype(bf16)

    owner, spot = code // 32, code % 32
    put_main = hot(jnp.where(spot < MAIN, owner * MAIN + spot, -1), experts * MAIN)
    ovf_row = jnp.where(spot >= MAIN, owner * ovf + spot - MAIN, -1)
    put_ovf = jnp.concatenate(
        [hot(jnp.where(ovf_row < 0, -1, ovf_row + j * extra), experts * ovf) for j in range(pieces)], axis=1
    )
    wide_rows = []
    for r, c in enumerate(codes):
        o, s = c // 32, c % 32
        inside = jnp.where(s < MAIN, r * MAIN + s, n_group * MAIN + r * extra + s - MAIN)
        wide_rows.append(o * chunk + inside)
    put_wide = hot(jnp.concatenate(wide_rows, axis=1), experts * chunk)

    payload = jnp.concatenate([inputs, cotang[:, :G_SLOT_COLS]], axis=1)
    w_a = payload.shape[1]
    q = w_a // pieces
    stacked = jnp.concatenate([payload[:, j * q : (j + 1) * q] for j in range(pieces)], axis=0)
    send_main = dot(put_main, payload).astype(bf16).reshape(experts, MAIN, w_a)
    send_ovf = dot(put_ovf, stacked).astype(bf16).reshape(experts, ovf, q)
    got_main = exchanged(send_main).reshape(experts * MAIN, w_a)
    got_ovf = exchanged(send_ovf).reshape(experts * ovf, q)
    pick_r = jnp.arange(experts * extra, dtype=jnp.int32)
    pick_c = jnp.arange(experts * ovf, dtype=jnp.int32)
    picks = [
        ((pick_r // extra * ovf + j * extra + pick_r % extra)[:, None] == pick_c[None, :]).astype(bf16)
        for j in range(pieces)
    ]
    ovf_rows = jnp.concatenate([dot(p, got_ovf).astype(bf16) for p in picks], axis=1)
    slot_blocks = gathered_x(jnp.concatenate([got_main, ovf_rows], axis=0))

    raw = jnp.concatenate(gathered_x(cotang[:, G_SLOT_COLS:]), axis=0)
    w_b = raw.shape[1]
    got_wide = exchanged(dot(put_wide, raw).astype(bf16).reshape(experts, chunk, w_b))
    n_main = n_group * MAIN

    def by_group(wide):
        w = wide.shape[-1]
        main = wide[:, :n_main].reshape(experts, n_group, MAIN, w).transpose(1, 0, 2, 3)
        rest = wide[:, n_main:].reshape(experts, n_group, extra, w).transpose(1, 0, 2, 3)
        return jnp.concatenate(
            [main.reshape(n_group, experts * MAIN, w), rest.reshape(n_group, experts * extra, w)], axis=1
        )

    def by_source(rows):
        w = rows.shape[-1]
        main = rows[:, : experts * MAIN].reshape(n_group, experts, MAIN, w).transpose(1, 0, 2, 3)
        rest = rows[:, experts * MAIN :].reshape(n_group, experts, extra, w).transpose(1, 0, 2, 3)
        return jnp.concatenate(
            [main.reshape(experts, n_main, w), rest.reshape(experts, n_group * extra, w)], axis=1
        )

    n_rows = n_group * experts * capacity
    rows_a = jnp.concatenate(slot_blocks, axis=0)
    rows_in = rows_a[:, :width]
    rows_cot = jnp.concatenate([rows_a[:, width:], by_group(got_wide).reshape(n_rows, w_b)], axis=1)

    logits = dot(rows_in, router_w)
    exp_logit = jnp.exp(logits)
    prob_rows = exp_logit / jnp.sum(exp_logit, axis=-1, keepdims=True)
    me = lax.axis_index("expert")
    mine = (jnp.arange(experts, dtype=jnp.int32) == me).astype(f32)[None, :]
    gate_val = jnp.sum(prob_rows * mine, axis=1, keepdims=True)
    scaled = routed_scale * gate_val.astype(bf16).astype(f32)
    hidden = dot(rows_in, gate_w)
    up_value = dot(rows_in, up_w)
    back_proj = dot(rows_cot, down_w, ((1,), (1,)))
    sigmoid_h = jax.nn.sigmoid(hidden)
    silu_val = hidden * sigmoid_h
    silu_slope = sigmoid_h * (1.0 + hidden * (1.0 - sigmoid_h))
    product = silu_val * up_value
    gate_part = jnp.sum(product * back_proj, axis=1, keepdims=True)
    grad_act = scaled * back_proj
    d_hidden = (grad_act * up_value * silu_slope).astype(bf16)
    d_up = (grad_act * silu_val).astype(bf16)
    g_act = (scaled * product).astype(bf16)
    d_logit = (routed_scale * gate_part * prob_rows * (mine - gate_val)).astype(bf16)
    partial = dot(d_hidden, gate_w, ((1,), (1,))) + dot(d_up, up_w, ((1,), (1,)))
    partial = (partial + dot(d_logit, router_w, ((1,), (1,)))).astype(bf16)
    router_part = dot(d_logit, rows_in, ((0,), (0,)))
    router_total = summed(router_part)

    blocks = partial.reshape(n_group, experts * capacity, width)
    wide_back = exchanged(by_source(blocks[:, :, P_SLOT_COLS:]))
    wide_back = wide_back.reshape(experts * chunk, width - P_SLOT_COLS)
    sums = scattered_x([blocks[r, :, :P_SLOT_COLS] for r in range(n_group)]).astype(bf16)
    back_main = exchanged(sums[: experts * MAIN].reshape(experts, MAIN, P_SLOT_COLS))
    qb = P_SLOT_COLS // pieces
    back_ovf = sum(
        dot(picks[j], sums[experts * MAIN :, j * qb : (j + 1) * qb], ((0,), (0,))) for j in range(pieces)
    ).astype(bf16)
    back_ovf = exchanged(back_ovf.reshape(experts, ovf, qb)).reshape(experts * ovf, qb)
    tok_wide = dot(put_wide, wide_back, ((0,), (0,))).astype(bf16).reshape(n_group, tok, -1)
    tok_b = scattered_x([tok_wide[r] for r in range(n_group)])
    tok_a = dot(put_main, back_main.reshape(experts * MAIN, P_SLOT_COLS), ((0,), (0,)))
    ovf_tok = dot(put_ovf, back_ovf, ((0,), (0,)))
    tok_a = tok_a + jnp.concatenate([ovf_tok[j * tok : (j + 1) * tok] for j in range(pieces)], axis=1)
    cot_out = (cotang.astype(f32) + jnp.concatenate([tok_a, tok_b], axis=1)).astype(bf16)
    n_sec = lax.axis_size("section")
    passed = lax.ppermute(cot_out, "section", [((i + 1) % n_sec, i) for i in range(n_sec)])

    grad_down = dot(g_act, rows_cot, ((0,), (0,))).astype(bf16)
    grad_gate = dot(rows_in, d_hidden, ((0,), (0,))).astype(bf16)
    grad_up = dot(rows_in, d_up, ((0,), (0,))).astype(bf16)
    return (
        passed[None],
        router_total.T[None],
        grad_gate[None, None],
        grad_up[None, None],
        grad_down[None, None],
    )


def solution(mesh):
    return jax.shard_map(
        on_device,
        mesh=mesh,
        in_specs=(
            P("section", ("expert", "tensor"), None),
            P("section", ("expert", "tensor"), None),
            P("section", None, None),
            P("section", "expert", None, "tensor"),
            P("section", "expert", None, "tensor"),
            P("section", "expert", "tensor", None),
            P("section", ("expert", "tensor"), None),
        ),
        out_specs=(
            P("section", ("expert", "tensor"), None),
            P("section", None, None),
            P("section", "expert", None, "tensor"),
            P("section", "expert", None, "tensor"),
            P("section", "expert", "tensor", None),
        ),
        check_vma=False,
    )
```

```python
import functools

import jax
import jax.numpy as jnp
from jax import lax
from jax.experimental import pallas as pl
from jax.experimental.pallas import tpu as pltpu
from jax.sharding import PartitionSpec as P

routed_scale = 16.0
MAIN = 16
EXTRA = 2
G_SLOT_COLS = 512
P_SLOT_COLS = 1536
P_PIECE = 256
VMEM_BYTES = 48 * 2**20
bf16 = jnp.bfloat16
f32 = jnp.float32
i32 = jnp.int32


def along_x(block, step):
    n = lax.axis_size("tensor")
    return lax.ppermute(block, "tensor", [(i, (i + step) % n) for i in range(n)])


def along_plane(block, step_y, step_z):
    n = lax.axis_size("expert")
    side = int(round(n**0.5))
    route = [
        (y * side + z, (y + step_y) % side * side + (z + step_z) % side)
        for y in range(side)
        for z in range(side)
    ]
    return lax.ppermute(block, "expert", route)


def gathered_x(block):
    half = block.shape[0] // 2
    above = along_x(block, -1)
    below = along_x(block, 1)
    far = jnp.concatenate([along_x(above[:half], -1), along_x(below[half:], 1)])
    return [block, above, far, below]


def add(a, b):
    return (a.astype(f32) + b.astype(f32)).astype(bf16)


def scattered_x(parts):
    own, up, far, down = parts
    half = own.shape[0] // 2
    from_below = along_x(far[:half], 1)
    from_above = along_x(far[half:], -1)
    up = jnp.concatenate([add(up[:half], from_below), up[half:]])
    down = jnp.concatenate([down[:half], add(down[half:], from_above)])
    return own.astype(f32) + along_x(up, 1).astype(f32) + along_x(down, -1).astype(f32)


def summed(block):
    for shift in (
        along_x,
        lambda b, d: along_plane(b, d, 0),
        lambda b, d: along_plane(b, 0, d),
    ):
        block = block + shift(block, 1) + shift(block, 2) + shift(block, 3)
    return block


def exchanged(block):
    return lax.all_to_all(block, "expert", split_axis=0, concat_axis=0, tiled=True)


def dot(a, b, contract=((1,), (0,))):
    return lax.dot_general(a, b, (contract, ((), ())), preferred_element_type=f32)


def iota(shape, dim):
    return lax.broadcasted_iota(i32, shape, dim)


def send_kernel(g_cols, pieces, ids_ref, x_ref, g_ref, out_ref, spot_ref):
    experts, tok = spot_ref.shape
    width = x_ref.shape[1] + g_cols
    piece = width // pieces
    e = iota((experts, tok), 0)
    hot = (ids_ref[0:1] == e) | (ids_ref[1:2] == e)
    earlier = (iota((tok, tok), 0) < iota((tok, tok), 1)).astype(bf16)
    spot = jnp.where(hot, dot(hot.astype(bf16), earlier), -1.0)
    spot_ref[...] = spot.astype(bf16)
    n = experts * MAIN
    spots = jnp.broadcast_to(spot[:, None, :], (experts, MAIN, tok)).reshape(n, tok).astype(i32)
    slot = iota((n, tok), 0) % MAIN
    put = (spots == slot).astype(bf16)
    payload = jnp.concatenate([x_ref[...], g_ref[:, :g_cols]], axis=1)
    out_ref[:, :width] = dot(put, payload).astype(bf16)
    total = jnp.zeros((n, piece), f32)
    for j in range(pieces):
        put = ((spots == MAIN + slot - j * EXTRA) & (slot // EXTRA == j)).astype(bf16)
        total = total + dot(put, payload[:, j * piece : (j + 1) * piece])
    out_ref[:, width:] = total.astype(bf16)


def send_slots(ids, x, g, experts, pieces):
    tok, width = x.shape[0], x.shape[1] + G_SLOT_COLS
    n = experts * MAIN
    return pl.pallas_call(
        functools.partial(send_kernel, G_SLOT_COLS, pieces),
        out_shape=(
            jax.ShapeDtypeStruct((n, width + width // pieces), bf16),
            jax.ShapeDtypeStruct((experts, tok), bf16),
        ),
        compiler_params=pltpu.CompilerParams(vmem_limit_bytes=VMEM_BYTES),
        cost_estimate=pl.CostEstimate(flops=2 * n * tok * width * 2, bytes_accessed=4 * 2**20, transcendentals=0),
    )(ids, x, g)


def rows_kernel(n_parts, g_cols, pieces, *refs):
    parts, (gate_ref, up_ref, router_ref, mine_ref) = refs[:n_parts], refs[n_parts : n_parts + 4]
    x_ref, g_ref, h_ref, u_ref, base_ref, scale_ref = refs[-6:]
    width = x_ref.shape[2]
    full = width + g_cols
    piece = full // pieces
    n = sum(p.shape[0] for p in parts)
    experts = n // MAIN
    rest = experts * EXTRA
    at = 0
    for p in parts:
        m = p.shape[0]
        x_ref[0, at : at + m] = p[:, :width]
        g_ref[0, at : at + m] = p[:, width:full]
        at += m
    packed = jnp.concatenate([p[:, full:] for p in parts], axis=0)
    a = iota((pieces * rest, n), 0)
    source = a % rest // EXTRA * MAIN + a // rest * EXTRA + a % EXTRA
    pick = (source == iota((pieces * rest, n), 1)).astype(bf16)
    spread = dot(pick, packed).astype(bf16)
    extra = jnp.concatenate([spread[j * rest : (j + 1) * rest] for j in range(pieces)], axis=1)
    x_ref[0, n:] = extra[:, :width]
    g_ref[0, n:] = extra[:, width:]
    x = x_ref[0]
    h_ref[0] = dot(x, gate_ref[...])
    u_ref[0] = dot(x, up_ref[...])
    exp_logit = jnp.exp(dot(x, router_ref[...], ((1,), (1,))))
    prob = exp_logit / jnp.sum(exp_logit, axis=1, keepdims=True)
    gate = jnp.sum(prob * mine_ref[...], axis=1, keepdims=True)
    base_ref[0] = routed_scale * prob * (mine_ref[...] - gate)
    scale_ref[0] = routed_scale * gate.astype(bf16).astype(f32)


def slot_rows(parts, weights, shapes, at, before, pieces):
    def block(s):
        return pl.BlockSpec((1, *s.shape[1:]), lambda i: (at, 0, 0))

    def whole(a):
        return pl.BlockSpec(a.shape, lambda i: (0,) * a.ndim)

    n_in = len(parts) + len(weights)
    rows, width = shapes[0].shape[1:]
    return pl.pallas_call(
        functools.partial(rows_kernel, len(parts), G_SLOT_COLS, pieces),
        grid=(1,),
        out_shape=shapes,
        in_specs=[whole(a) for a in (*parts, *weights)] + [pl.BlockSpec(memory_space=pl.ANY)] * len(before),
        out_specs=[block(s) for s in shapes],
        input_output_aliases={n_in + i: i for i in range(len(before))},
        compiler_params=pltpu.CompilerParams(vmem_limit_bytes=VMEM_BYTES),
        cost_estimate=pl.CostEstimate(
            flops=2 * rows * width * 1024, bytes_accessed=10 * 2**20, transcendentals=rows * 16
        ),
    )(*parts, *weights, *before)


def back_kernel(n_group, cols, piece, *refs):
    (gs_ref, wide_ref, rest_ref, h_ref, u_ref, base_ref, scale_ref, gate_ref, up_ref, down_ref, router_ref) = refs[:11]
    (g_ref, dh_ref, du_ref, ga_ref, dl_ref, pa_ref, pb_ref, total) = refs[11:]
    r = pl.program_id(0)
    experts = wide_ref.shape[0]
    n = experts * MAIN
    rest = experts * EXTRA
    group_rest = n_group * EXTRA
    first = gs_ref.shape[2]
    width = g_ref.shape[2]

    def where_rest(a):
        return a // EXTRA * group_rest + r * EXTRA + a % EXTRA

    shape = (rest, experts * group_rest)
    pick = (where_rest(iota(shape, 0)) == iota(shape, 1)).astype(bf16)
    g_ref[0, :, :first] = gs_ref[0]
    g_ref[0, :n, first:] = wide_ref[...].reshape(n, width - first)
    g_ref[0, n:, first:] = dot(pick, rest_ref[...]).astype(bf16)
    e = dot(g_ref[0], down_ref[...], ((1,), (1,)))
    hidden, up_value, scaled = h_ref[0], u_ref[0], scale_ref[0]
    sig = 1.0 / (1.0 + jnp.exp(-hidden))
    silu = hidden * sig
    product = silu * up_value
    part = jnp.sum(product * e, axis=1, keepdims=True)
    grad = scaled * e
    dh = (grad * up_value * (sig * (1.0 + hidden * (1.0 - sig)))).astype(bf16)
    du = (grad * silu).astype(bf16)
    dl = (part * base_ref[0]).astype(bf16)
    dh_ref[0], du_ref[0], dl_ref[0] = dh, du, dl
    ga_ref[0] = (scaled * product).astype(bf16)

    pieces = -(-cols // piece)
    step = 512
    extra = []
    shape_t = (experts * group_rest, rest)
    pick_t = (iota(shape_t, 0) == where_rest(iota(shape_t, 1))).astype(bf16)
    for c in range(0, width, step):
        at = slice(c, c + step)
        p = dot(dh, gate_ref[at], ((1,), (1,))) + dot(du, up_ref[at], ((1,), (1,))) + dot(dl, router_ref[:, at])
        p = p.astype(bf16)
        if c < cols:
            pa_ref[0, :, at] = p[:n]
            extra += [p[n:, k : k + piece] for k in range(0, step, piece)]
        else:
            pb_ref[:, pl.ds(pl.multiple_of(r * MAIN, MAIN), MAIN), c - cols : c - cols + step] = p[:n].reshape(
                experts, MAIN, step
            )
            more = dot(pick_t, p[n:])
            to = slice(c - cols, c - cols + step)
            total[:, to] = jnp.where(r == 0, more, total[:, to] + more)
    a = iota((n, pieces * rest), 1)
    goes = a % rest // EXTRA * MAIN + a // rest * EXTRA + a % EXTRA
    pack = (iota((n, pieces * rest), 0) == goes).astype(bf16)
    pa_ref[0, :, cols:] = dot(pack, jnp.concatenate(extra, axis=0)).astype(bf16)

    @pl.when(r == n_group - 1)
    def _():
        pb_ref[:, n_group * MAIN :, :] = total[...].reshape(experts, group_rest, -1).astype(bf16)


def owner_back(slots, wide, rest_rows, weights, n_group):
    _, gs, h, u, base, scale = slots
    gate_w, up_w, down_w, router_t = weights
    rows, ff = h.shape[1:]
    width = gate_w.shape[0]
    experts = wide.shape[0]
    chunk = n_group * (MAIN + EXTRA)
    n = experts * MAIN

    def block(a):
        return pl.BlockSpec((1, *a.shape[1:]), lambda r: (r, 0, 0))

    def whole(a):
        return pl.BlockSpec(a.shape, lambda r: (0,) * a.ndim)

    s = jax.ShapeDtypeStruct
    out = (
        s((n_group, rows, width), bf16),
        s((n_group, rows, ff), bf16),
        s((n_group, rows, ff), bf16),
        s((n_group, rows, ff), bf16),
        s((n_group, rows, experts), bf16),
        s((n_group, n, P_SLOT_COLS + P_PIECE), bf16),
        s((experts, chunk, width - P_SLOT_COLS), bf16),
    )
    return pl.pallas_call(
        functools.partial(back_kernel, n_group, P_SLOT_COLS, P_PIECE),
        grid=(n_group,),
        out_shape=out,
        in_specs=[
            block(gs),
            pl.BlockSpec((experts, MAIN, wide.shape[2]), lambda r: (0, r, 0)),
            whole(rest_rows),
            block(h),
            block(u),
            block(base),
            block(scale),
            whole(gate_w),
            whole(up_w),
            whole(down_w),
            whole(router_t),
        ],
        out_specs=[block(a) for a in out[:6]] + [whole(out[6])],
        scratch_shapes=[pltpu.VMEM((experts * n_group * EXTRA, width - P_SLOT_COLS), f32)],
        compiler_params=pltpu.CompilerParams(vmem_limit_bytes=VMEM_BYTES),
        cost_estimate=pl.CostEstimate(
            flops=6 * n_group * rows * width * ff, bytes_accessed=30 * 2**20, transcendentals=n_group * rows * ff
        ),
    )(gs, wide, rest_rows, h, u, base, scale, gate_w, up_w, down_w, router_t)


def on_device(saved_inputs, out_cotangent, router, w_gate, w_up, w_down, expert_ids):
    inputs, cotang, router_t = saved_inputs[0], out_cotangent[0], router[0].T
    gate_w, up_w, down_w = w_gate[0, 0], w_up[0, 0], w_down[0, 0]
    experts = lax.axis_size("expert")
    n_group = lax.axis_size("tensor")
    tok, width = inputs.shape
    chunk = n_group * (MAIN + EXTRA)
    n_main = experts * MAIN
    pieces = MAIN // EXTRA
    rows = experts * (MAIN + EXTRA)
    ff = gate_w.shape[1]
    cols = P_SLOT_COLS

    send, spot = send_slots(expert_ids[0].T, inputs, cotang, experts, pieces)
    got = exchanged(send.reshape(experts, MAIN, -1)).reshape(n_main, -1)
    raw = jnp.concatenate(gathered_x(cotang[:, G_SLOT_COLS:]), axis=0)
    spots = [spot, along_x(spot, -1), along_x(spot, 2), along_x(spot, 1)]
    inside = []
    for r, s in enumerate(spots):
        s = s.astype(i32)
        at = jnp.where(s < MAIN, r * MAIN + s, n_group * MAIN + r * EXTRA + s - MAIN)
        inside.append(jnp.where(s < 0, -1, at))
    inside = jnp.concatenate(inside, axis=1)
    put_wide = (inside[:, None, :] == jnp.arange(chunk, dtype=i32)[None, :, None]).astype(bf16)
    put_wide = put_wide.reshape(experts * chunk, n_group * tok)
    got_wide = exchanged(dot(put_wide, raw).astype(bf16).reshape(experts, chunk, -1))
    rest_wide = got_wide[:, n_group * MAIN :].reshape(experts * n_group * EXTRA, -1)

    mine = (jnp.arange(experts, dtype=i32) == lax.axis_index("expert")).astype(f32)[None, :]
    weights = (gate_w, up_w, router_t, mine)
    s = jax.ShapeDtypeStruct
    shapes = (
        s((n_group, rows, width), bf16),
        s((n_group, rows, G_SLOT_COLS), bf16),
        s((n_group, rows, ff), f32),
        s((n_group, rows, ff), f32),
        s((n_group, rows, experts), f32),
        s((n_group, rows, 1), f32),
    )
    half = n_main // 2
    above, below = along_x(got, -1), along_x(got, 1)
    far = (along_x(above[:half], -1), along_x(below[half:], 1))
    slots = slot_rows((got,), weights, shapes, 0, (), pieces)
    slots = slot_rows((above,), weights, shapes, 1, slots, pieces)
    slots = slot_rows((below,), weights, shapes, 3, slots, pieces)
    slots = slot_rows(far, weights, shapes, 2, slots, pieces)

    rows_cot, d_hidden, d_up, g_act, d_logit, part_a, part_b = owner_back(
        slots, got_wide, rest_wide, (gate_w, up_w, down_w, router_t), n_group
    )
    n_rows = n_group * rows
    rows_in, rows_cot = slots[0].reshape(n_rows, width), rows_cot.reshape(n_rows, width)
    d_hidden, d_up, g_act = (a.reshape(n_rows, ff) for a in (d_hidden, d_up, g_act))

    wide_back = exchanged(part_b).reshape(experts * chunk, width - cols)
    sums = scattered_x([part_a[r] for r in range(n_group)]).astype(bf16)
    back = exchanged(sums.reshape(experts, MAIN, -1)).reshape(n_main, -1)
    router_total = summed(dot(d_logit.reshape(n_rows, experts), rows_in, ((0,), (0,))))

    tok_wide = dot(put_wide, wide_back, ((0,), (0,))).astype(bf16).reshape(n_group, tok, -1)
    tok_b = scattered_x([tok_wide[r] for r in range(n_group)])
    own = jnp.broadcast_to(spot.astype(i32)[:, None, :], (experts, MAIN, tok)).reshape(n_main, tok)
    slot = (jnp.arange(n_main, dtype=i32) % MAIN)[:, None]
    tok_a = dot((own == slot).astype(bf16), back[:, :cols], ((0,), (0,)))
    p_pieces = -(-cols // P_PIECE)
    folded = [(own == MAIN + slot - j * EXTRA) & (slot // EXTRA == j) for j in range(p_pieces)]
    folded = jnp.concatenate(folded, axis=1).astype(bf16)
    unfolded = dot(folded, back[:, cols:], ((0,), (0,)))
    tok_a = tok_a + jnp.concatenate([unfolded[j * tok : (j + 1) * tok] for j in range(p_pieces)], axis=1)
    cot_out = (cotang.astype(f32) + jnp.concatenate([tok_a, tok_b], axis=1)).astype(bf16)
    n_sec = lax.axis_size("section")
    passed = lax.ppermute(cot_out, "section", [((i + 1) % n_sec, i) for i in range(n_sec)])

    grad_down = dot(g_act, rows_cot, ((0,), (0,))).astype(bf16)
    grad_gate = dot(rows_in, d_hidden, ((0,), (0,))).astype(bf16)
    grad_up = dot(rows_in, d_up, ((0,), (0,))).astype(bf16)
    return (
        passed[None],
        router_total.T[None],
        grad_gate[None, None],
        grad_up[None, None],
        grad_down[None, None],
    )


def solution(mesh):
    return jax.shard_map(
        on_device,
        mesh=mesh,
        in_specs=(
            P("section", ("expert", "tensor"), None),
            P("section", ("expert", "tensor"), None),
            P("section", None, None),
            P("section", "expert", None, "tensor"),
            P("section", "expert", None, "tensor"),
            P("section", "expert", "tensor", None),
            P("section", ("expert", "tensor"), None),
        ),
        out_specs=(
            P("section", ("expert", "tensor"), None),
            P("section", None, None),
            P("section", "expert", None, "tensor"),
            P("section", "expert", None, "tensor"),
            P("section", "expert", "tensor", None),
        ),
        check_vma=False,
    )
```

```python
import functools

import jax
import jax.numpy as jnp
from jax import lax
from jax.experimental import pallas as pl
from jax.experimental.pallas import tpu as pltpu
from jax.sharding import PartitionSpec as P

routed_scale = 16.0
MAIN = 16
EXTRA = 2
G_SLOT_COLS = 512
P_SPLIT = 1024
STEP = 512
VMEM_BYTES = 60 * 2**20
SMALL_VMEM = 28 * 2**20
bf16 = jnp.bfloat16
f32 = jnp.float32
i32 = jnp.int32


def along_x(block, step):
    n = lax.axis_size("tensor")
    return lax.ppermute(block, "tensor", [(i, (i + step) % n) for i in range(n)])


def along_plane(block, step_y, step_z):
    n = lax.axis_size("expert")
    side = int(round(n**0.5))
    route = [
        (y * side + z, (y + step_y) % side * side + (z + step_z) % side)
        for y in range(side)
        for z in range(side)
    ]
    return lax.ppermute(block, "expert", route)


def gathered_x(block):
    half = block.shape[0] // 2
    above = along_x(block, -1)
    below = along_x(block, 1)
    return block, above, along_x(above[:half], -1), along_x(below[half:], 1), below


def add(a, b):
    return (a.astype(f32) + b.astype(f32)).astype(bf16)


def ring_first(far_lo, far_hi, up_hi, down_lo):
    return along_x(far_lo, 1), along_x(far_hi, -1), along_x(up_hi, 1), along_x(down_lo, -1)


def ring_second(own, up_lo, down_hi, from_below, from_above, hi_below, lo_above):
    half = up_lo.shape[0]
    lo_below = along_x(add(up_lo, from_below), 1)
    hi_above = along_x(add(down_hi, from_above), -1)
    lo = own[:half].astype(f32) + lo_below.astype(f32) + lo_above.astype(f32)
    hi = own[half:].astype(f32) + hi_below.astype(f32) + hi_above.astype(f32)
    return jnp.concatenate([lo.astype(bf16), hi.astype(bf16)], axis=0)


def along_y(block, step):
    return along_plane(block, step, 0)


def along_z(block, step):
    return along_plane(block, 0, step)


def ring_total(block, shift):
    return block + shift(block, 1) + shift(block, 2) + shift(block, 3)


def exchanged(block):
    return lax.all_to_all(block, "expert", split_axis=0, concat_axis=0, tiled=True)


def dot(a, b, contract=((1,), (0,))):
    return lax.dot_general(a, b, (contract, ((), ())), preferred_element_type=f32)


def iota(shape, dim):
    return lax.broadcasted_iota(i32, shape, dim)


def spread_spots(spot):
    experts, tok = spot.shape
    n = experts * MAIN
    return jnp.broadcast_to(spot[:, None, :], (experts, MAIN, tok)).reshape(n, tok).astype(i32)


def put_slot(spots):
    return (spots == iota(spots.shape, 0) % MAIN).astype(bf16)


def put_folded(spots, j):
    slot = iota(spots.shape, 0) % MAIN
    return ((spots == MAIN + slot - j * EXTRA) & (slot // EXTRA == j)).astype(bf16)


def place(spots, payload, pieces):
    piece = payload.shape[1] // pieces
    total = jnp.zeros((spots.shape[0], piece), f32)
    for j in range(pieces):
        total = total + dot(put_folded(spots, j), payload[:, j * piece : (j + 1) * piece])
    return dot(put_slot(spots), payload).astype(bf16), total.astype(bf16)


def unfold(packed, pieces):
    n = packed.shape[0]
    rest = n // MAIN * EXTRA
    a = iota((pieces * rest, n), 0)
    source = a % rest // EXTRA * MAIN + a // rest * EXTRA + a % EXTRA
    spread = dot((source == iota((pieces * rest, n), 1)).astype(bf16), packed).astype(bf16)
    return jnp.concatenate([spread[j * rest : (j + 1) * rest] for j in range(pieces)], axis=1)


def fold(pieces, n):
    rest = n // MAIN * EXTRA
    a = iota((n, len(pieces) * rest), 1)
    goes = a % rest // EXTRA * MAIN + a // rest * EXTRA + a % EXTRA
    pack = (iota((n, len(pieces) * rest), 0) == goes).astype(bf16)
    return dot(pack, jnp.concatenate(pieces, axis=0)).astype(bf16)


def whole(a):
    return pl.BlockSpec(a.shape, lambda *i: (0,) * a.ndim)


def params(size=VMEM_BYTES):
    return pltpu.CompilerParams(vmem_limit_bytes=size)


def send_kernel(g_cols, pieces, ids_ref, x_ref, g_ref, out_ref, spot_ref, raw_ref):
    experts, tok = spot_ref.shape
    width = x_ref.shape[1] + g_cols
    e = iota((experts, tok), 0)
    hot = (ids_ref[0:1] == e) | (ids_ref[1:2] == e)
    earlier = (iota((tok, tok), 0) < iota((tok, tok), 1)).astype(bf16)
    spot = jnp.where(hot, dot(hot.astype(bf16), earlier), -1.0)
    spot_ref[...] = spot.astype(bf16)
    raw_ref[:, : raw_ref.shape[1] - tok] = g_ref[:, g_cols:]
    raw_ref[:, raw_ref.shape[1] - tok :] = jnp.concatenate([spot, jnp.zeros((tok - experts, tok), f32)], axis=0).T.astype(
        bf16
    )
    payload = jnp.concatenate([x_ref[...], g_ref[:, :g_cols]], axis=1)
    out_ref[:, :width], out_ref[:, width:] = place(spread_spots(spot), payload, pieces)


def send_slots(ids, x, g, experts, pieces):
    tok, width = x.shape[0], x.shape[1] + G_SLOT_COLS
    n = experts * MAIN
    s = jax.ShapeDtypeStruct
    return pl.pallas_call(
        functools.partial(send_kernel, G_SLOT_COLS, pieces),
        out_shape=(
            s((n, width + width // pieces), bf16),
            s((experts, tok), bf16),
            s((tok, g.shape[1] - G_SLOT_COLS + tok), bf16),
        ),
        compiler_params=params(),
        cost_estimate=pl.CostEstimate(flops=2 * n * tok * width * 2, bytes_accessed=4 * 2**20, transcendentals=0),
    )(ids, x, g)


def wide_kernel(pieces, own_ref, above_ref, far1_ref, far2_ref, below_ref, out_ref):
    experts = out_ref.shape[0]
    tok = own_ref.shape[0]
    width = own_ref.shape[1] - tok
    far = jnp.concatenate([far1_ref[...], far2_ref[...]], axis=0)
    for r, raw in enumerate((own_ref[...], above_ref[...], far, below_ref[...])):
        at = slice(r * MAIN, (r + 1) * MAIN)
        spot = raw[:, width:].astype(f32).T[:experts]
        main, folded = place(spread_spots(spot), raw[:, :width], pieces)
        out_ref[:, at, :width] = main.reshape(experts, MAIN, width)
        out_ref[:, at, width:] = folded.reshape(experts, MAIN, width // pieces)


def wide_slots(raws, n_group, experts, pieces):
    tok = raws[0].shape[0]
    width = raws[0].shape[1] - tok
    return pl.pallas_call(
        functools.partial(wide_kernel, pieces),
        out_shape=jax.ShapeDtypeStruct((experts, n_group * MAIN, width + width // pieces), bf16),
        compiler_params=params(SMALL_VMEM),
        cost_estimate=pl.CostEstimate(
            flops=2 * experts * MAIN * n_group * tok * width * 2, bytes_accessed=8 * 2**20, transcendentals=0
        ),
    )(*raws)


def lay_out(parts, width, full, pieces, x_ref, g_ref):
    n = sum(p.shape[0] for p in parts)
    at = 0
    for p in parts:
        m = p.shape[0]
        x_ref[0, at : at + m] = p[:, :width]
        g_ref[0, at : at + m] = p[:, width:full]
        at += m
    extra = unfold(jnp.concatenate([p[:, full:] for p in parts], axis=0), pieces)
    x_ref[0, n:] = extra[:, :width]
    g_ref[0, n:] = extra[:, width:]


def x_part(x, w_refs, router_ref, mine_ref, h_ref, u_ref, aux_ref):
    experts = router_ref.shape[0]
    ff = h_ref.shape[2]
    both = jnp.concatenate([dot(x, w[...]) for w in w_refs], axis=1)
    h_ref[0] = both[:, :ff]
    u_ref[0] = both[:, ff:]
    exp_logit = jnp.exp(dot(x, router_ref[...], ((1,), (1,))))
    prob = exp_logit / jnp.sum(exp_logit, axis=1, keepdims=True)
    gate = jnp.sum(prob * mine_ref[...], axis=1, keepdims=True)
    base = routed_scale * prob * (mine_ref[...] - gate)
    scale = routed_scale * gate.astype(bf16).astype(f32)
    aux_ref[0] = jnp.concatenate([base, jnp.broadcast_to(scale, base.shape)], axis=1)


def rows_kernel(g_cols, pieces, n_parts, *refs):
    gate_ref, up_ref, router_ref, mine_ref = refs[n_parts : n_parts + 4]
    x_ref, g_ref, h_ref, u_ref, aux_ref = refs[-5:]
    width = x_ref.shape[2]
    lay_out(refs[:n_parts], width, width + g_cols, pieces, x_ref, g_ref)
    x_part(x_ref[0], (gate_ref, up_ref), router_ref, mine_ref, h_ref, u_ref, aux_ref)


def slot_rows(parts, weights, shapes, at, before, pieces):
    def block(s):
        return pl.BlockSpec((1, *s.shape[1:]), lambda i: (at, 0, 0))

    rows, width = shapes[0].shape[1:]
    args = (*parts, *weights)
    return pl.pallas_call(
        functools.partial(rows_kernel, G_SLOT_COLS, pieces, len(parts)),
        grid=(1,),
        out_shape=shapes,
        in_specs=[whole(a) for a in args] + [pl.BlockSpec(memory_space=pl.ANY)] * len(before),
        out_specs=[block(s) for s in shapes],
        input_output_aliases={len(args) + i: i for i in range(len(before))},
        compiler_params=params(),
        cost_estimate=pl.CostEstimate(
            flops=2 * rows * width * 1024, bytes_accessed=10 * 2**20, transcendentals=rows * 16
        ),
    )(*args, *before)


def turned(w_back, w_in, router):
    ff2 = w_in.shape[1]
    w_back[:ff2] = w_in.T
    pad = jnp.zeros((w_back.shape[0] - ff2 - router.shape[0], router.shape[1]), bf16)
    w_back[ff2:] = jnp.concatenate([router, pad], axis=0)


def send_back(d, w_back, pa, out_refs, sems):
    n_group, n, total = pa.shape
    cols = w_back.shape[1]
    piece = total - cols
    rows = d.shape[0] // n_group
    half = n // 2
    lo, hi = slice(0, half), slice(half, n)
    parts = ((0, slice(0, n)), (2, lo), (2, hi), (1, lo), (1, hi), (3, lo), (3, hi))
    out = []

    def send(at, k):
        for j, ((q, part), to) in enumerate(zip(parts, out_refs)):
            out.append(pltpu.make_async_copy(pa.at[q, part, at], to.at[:, at], sems.at[k, j]))
            out[-1].start()

    extra = [[] for _ in range(n_group)]
    for k, c in enumerate(range(0, cols, STEP)):
        at = slice(c, c + STEP)
        p = dot(d, w_back[:, at]).astype(bf16)
        for q in range(n_group):
            pa[q, :, at] = p[q * rows : q * rows + n]
            extra[q] += [p[q * rows + n : (q + 1) * rows, j : j + piece] for j in range(0, STEP, piece)]
        send(at, k)
    for q in range(n_group):
        pa[q, :, cols:] = fold(extra[q], n)
    send(slice(cols, total), cols // STEP)
    for c in out:
        c.wait()


def back_shapes(n, cols, piece):
    s = jax.ShapeDtypeStruct
    return (s((n, cols + piece), bf16),) + (s((n // 2, cols + piece), bf16),) * 6


def piece_of(cols):
    return -(-cols // (MAIN // EXTRA * 128)) * 128


def whole_rows(g, slot_cols, wide_ref, pieces):
    first = slot_cols.shape[1]
    n = wide_ref.shape[0] * MAIN
    wide = g.shape[1] - first
    g[:, :first] = slot_cols
    g[:n, first:] = wide_ref[:, :, :wide].reshape(n, wide)
    g[n:, first:] = unfold(wide_ref[:, :, wide:].reshape(n, wide // pieces), pieces)


def back_kernel(n_group, x_pieces, wide_pieces, *refs):
    (gs_ref, wide_ref, h_ref, u_ref, aux_ref, router_ref, mine_ref) = refs[:7]
    from_refs = refs[7:12]
    x, ga_ref, d_ref = refs[13:16]
    out_refs = refs[16:23]
    g, hs, us, axs, gs, down_ref, w_in_ref, far1_ref, far2_ref, w_back, pa, in_sems, a_sems = refs[23:]
    i = pl.program_id(0)
    last = n_group - 1
    r = i + (i == 2).astype(i32) - (i == 3).astype(i32)
    experts = wide_ref.shape[0]
    n = experts * MAIN
    first = gs_ref.shape[2]
    width = g.shape[1]
    ff = h_ref.shape[2]
    rows = h_ref.shape[1]
    cols = w_back.shape[1]
    lands = (down_ref, w_in_ref.at[:, :ff], w_in_ref.at[:, ff:], far1_ref, far2_ref)
    copies = [pltpu.make_async_copy(s, d, in_sems.at[k]) for k, (s, d) in enumerate(zip(from_refs, lands))]

    @pl.when(i == 0)
    def _():
        for c in copies:
            c.start()
        copies[0].wait()

    @pl.when(i < last)
    def _():
        hs[...], us[...], axs[...], gs[...] = h_ref[...], u_ref[...], aux_ref[...], gs_ref[...]

    @pl.when(i == last)
    def _():
        copies[3].wait()
        copies[4].wait()
        lay_out((far1_ref, far2_ref), width, width + first, x_pieces, x, gs)
        x_part(x[0], (w_in_ref,), router_ref, mine_ref, hs, us, axs)

    whole_rows(g, gs[0], wide_ref, wide_pieces)
    e = dot(g[...], down_ref[...], ((1,), (1,)))
    hidden, up_value = hs[0], us[0]
    base, scaled = axs[0, :, :experts], axs[0, :, experts : experts + 1]
    sig = 1.0 / (1.0 + jnp.exp(-hidden))
    silu = hidden * sig
    product = silu * up_value
    part = jnp.sum(product * e, axis=1, keepdims=True)
    grad = scaled * e
    dh = (grad * up_value * (sig * (1.0 + hidden * (1.0 - sig)))).astype(bf16)
    du = (grad * silu).astype(bf16)
    dl = (part * base).astype(bf16)
    pad = jnp.zeros((rows, d_ref.shape[2] - 2 * ff - experts), bf16)
    d_ref[r] = jnp.concatenate([dh, du, dl, pad], axis=1)
    ga_ref[0] = (scaled * product).astype(bf16)

    @pl.when(i == 0)
    def _():
        copies[1].wait()
        copies[2].wait()
        turned(w_back, w_in_ref[:cols], router_ref[:, :cols])

    @pl.when(i == last)
    def _():
        d = d_ref[...].reshape(n_group * rows, d_ref.shape[2])
        send_back(d, w_back, pa, out_refs, a_sems)


def owner_back(slots, far, wide, weights, n_group, pieces, wide_pieces):
    x, gs, h, u, aux = slots
    gate_w, up_w, down_w, router_t, mine = weights
    rows, ff = h.shape[1:]
    width = x.shape[2]
    experts = wide.shape[0]
    n = experts * MAIN
    piece = piece_of(P_SPLIT)

    def turn(i):
        return i + (i == 2).astype(i32) - (i == 3).astype(i32)

    def block(a):
        return pl.BlockSpec((1, *a.shape[1:]), lambda i: (turn(i), 0, 0))

    s = jax.ShapeDtypeStruct
    out = (
        s(x.shape, bf16),
        s((n_group, rows, ff), bf16),
        s((n_group, rows, 2 * ff + 128), bf16),
        *back_shapes(n, P_SPLIT, piece),
    )
    later = (down_w, gate_w, up_w, *far)
    here = pl.BlockSpec(memory_space=pl.ANY)
    return pl.pallas_call(
        functools.partial(back_kernel, n_group, pieces, wide_pieces),
        grid=(n_group,),
        out_shape=out,
        in_specs=[
            block(gs),
            pl.BlockSpec((experts, MAIN, wide.shape[2]), lambda i: (0, turn(i), 0)),
            block(h),
            block(u),
            block(aux),
            whole(router_t),
            whole(mine),
        ]
        + [here] * (len(later) + 1),
        out_specs=[pl.BlockSpec((1, *x.shape[1:]), lambda i: (2, 0, 0)), block(out[1]), whole(out[2])]
        + [here] * 7,
        scratch_shapes=[
            pltpu.VMEM((rows, width), bf16),
            pltpu.VMEM((1, rows, ff), f32),
            pltpu.VMEM((1, rows, ff), f32),
            pltpu.VMEM((1, *aux.shape[1:]), f32),
            pltpu.VMEM((1, rows, gs.shape[2]), bf16),
            pltpu.VMEM(down_w.shape, bf16),
            pltpu.VMEM((width, 2 * ff), bf16),
            pltpu.VMEM(far[0].shape, bf16),
            pltpu.VMEM(far[1].shape, bf16),
            pltpu.VMEM((2 * ff + 128, P_SPLIT), bf16),
            pltpu.VMEM((n_group, n, P_SPLIT + piece), bf16),
            pltpu.SemaphoreType.DMA((len(later),)),
            pltpu.SemaphoreType.DMA((P_SPLIT // STEP + 1, 7)),
        ],
        input_output_aliases={12: 0},
        compiler_params=params(),
        cost_estimate=pl.CostEstimate(
            flops=6 * n_group * rows * width * ff, bytes_accessed=40 * 2**20, transcendentals=n_group * rows * ff
        ),
    )(gs, wide, h, u, aux, router_t, mine, *later, x)


def down_kernel(x_pieces, wide_pieces, gs_ref, wide_ref, ga_ref, far1_ref, far2_ref, out_ref, x, gs, g):
    r = pl.program_id(0)
    first = gs_ref.shape[2]
    n_group, rows, ff = ga_ref.shape
    width = g.shape[2]

    @pl.when(r == 2)
    def _():
        lay_out((far1_ref, far2_ref), width, width + first, x_pieces, x, gs)

    @pl.when(r != 2)
    def _():
        gs[...] = gs_ref[...]

    whole_rows(g.at[r], gs[0], wide_ref, wide_pieces)

    @pl.when(r == n_group - 1)
    def _():
        turned_act = ga_ref[...].reshape(n_group * rows, ff).T
        for c in range(0, width, STEP):
            at = slice(c, c + STEP)
            out_ref[:, at] = dot(turned_act, g[:, :, at].reshape(n_group * rows, STEP)).astype(bf16)


def down_gradient(width, gs, far, wide, g_act, pieces, wide_pieces):
    n_group, rows, ff = g_act.shape
    experts = wide.shape[0]
    out = jax.ShapeDtypeStruct((ff, width), bf16)
    return pl.pallas_call(
        functools.partial(down_kernel, pieces, wide_pieces),
        grid=(n_group,),
        out_shape=out,
        in_specs=[
            pl.BlockSpec((1, *gs.shape[1:]), lambda i: (i, 0, 0)),
            pl.BlockSpec((experts, MAIN, wide.shape[2]), lambda i: (0, i, 0)),
            whole(g_act),
            whole(far[0]),
            whole(far[1]),
        ],
        out_specs=whole(out),
        scratch_shapes=[
            pltpu.VMEM((1, rows, width), bf16),
            pltpu.VMEM((1, rows, gs.shape[2]), bf16),
            pltpu.VMEM((n_group, rows, width), bf16),
        ],
        compiler_params=params(),
        cost_estimate=pl.CostEstimate(
            flops=2 * n_group * rows * width * ff, bytes_accessed=16 * 2**20, transcendentals=0
        ),
    )(gs, wide, g_act, *far)


def x_kernel(experts, x_ref, d_ref, gate_ref, up_ref, router_ref):
    ff = gate_ref.shape[1]
    rows = x_ref.shape[0] * x_ref.shape[1]
    x = x_ref[...].reshape(rows, x_ref.shape[2])
    d = d_ref[...].reshape(rows, d_ref.shape[2])
    both = dot(x.T, d[:, : 2 * ff])
    gate_ref[...] = both[:, :ff].astype(bf16)
    up_ref[...] = both[:, ff:].astype(bf16)
    router_ref[...] = dot(d[:, 2 * ff :], x, ((0,), (0,)))[:experts]


def x_gradients(x_rows, d, ff, experts):
    n_group, rows, width = x_rows.shape
    s = jax.ShapeDtypeStruct
    return pl.pallas_call(
        functools.partial(x_kernel, experts),
        grid=(width // STEP,),
        out_shape=(s((width, ff), bf16), s((width, ff), bf16), s((experts, width), f32)),
        in_specs=[pl.BlockSpec((n_group, rows, STEP), lambda c: (0, 0, c)), whole(d)],
        out_specs=[
            pl.BlockSpec((STEP, ff), lambda c: (c, 0)),
            pl.BlockSpec((STEP, ff), lambda c: (c, 0)),
            pl.BlockSpec((experts, STEP), lambda c: (0, c)),
        ],
        compiler_params=params(),
        cost_estimate=pl.CostEstimate(
            flops=4 * n_group * rows * width * ff, bytes_accessed=12 * 2**20, transcendentals=0
        ),
    )(x_rows, d)


def rest_back_kernel(d_ref, gate_ref, up_ref, router_ref, *refs):
    out_refs = refs[:7]
    w_in, w_back, pa, in_sems, sems = refs[7:]
    n_group, rows = d_ref.shape[:2]
    ff = gate_ref.shape[1]
    cols = w_back.shape[1]
    first = gate_ref.shape[0] - cols
    copies = [
        pltpu.make_async_copy(w.at[pl.ds(first, cols)], w_in.at[:, k * ff : (k + 1) * ff], in_sems.at[k])
        for k, w in enumerate((gate_ref, up_ref))
    ]
    for c in copies:
        c.start()
    for c in copies:
        c.wait()
    turned(w_back, w_in[...], router_ref[:, first:])
    send_back(d_ref[...].reshape(n_group * rows, d_ref.shape[2]), w_back, pa, out_refs, sems)


def rest_back(d, gate_w, up_w, router_t):
    n_group, rows = d.shape[:2]
    width, ff = gate_w.shape
    n = router_t.shape[0] * MAIN
    cols = width - P_SPLIT
    piece = piece_of(cols)
    here = pl.BlockSpec(memory_space=pl.ANY)
    return pl.pallas_call(
        rest_back_kernel,
        out_shape=back_shapes(n, cols, piece),
        in_specs=[pl.BlockSpec(memory_space=pltpu.VMEM), here, here, pl.BlockSpec(memory_space=pltpu.VMEM)],
        out_specs=[here] * 7,
        scratch_shapes=[
            pltpu.VMEM((cols, 2 * ff), bf16),
            pltpu.VMEM((2 * ff + 128, cols), bf16),
            pltpu.VMEM((n_group, n, cols + piece), bf16),
            pltpu.SemaphoreType.DMA((2,)),
            pltpu.SemaphoreType.DMA((cols // STEP + 1, 7)),
        ],
        compiler_params=params(),
        cost_estimate=pl.CostEstimate(
            flops=4 * n_group * rows * ff * cols, bytes_accessed=12 * 2**20, transcendentals=0
        ),
    )(d, gate_w, up_w, router_t)


def finish_kernel(splits, spot_ref, cot_ref, *refs):
    out_ref = refs[-1]
    tok = cot_ref.shape[0]
    spots = spread_spots(spot_ref[...].astype(f32))
    main = put_slot(spots)
    folded = [put_folded(spots, j) for j in range(MAIN // EXTRA)]
    for (first, cols), back_ref in zip(splits, refs[:-1]):
        q = back_ref.shape[1] - cols
        pieces = cols // q
        rows = dot(main, back_ref[:, :cols], ((0,), (0,)))
        more = dot(jnp.concatenate(folded[:pieces], axis=1), back_ref[:, cols:], ((0,), (0,)))
        for j in range(pieces):
            at = slice(j * q, (j + 1) * q)
            to = slice(first + j * q, first + (j + 1) * q)
            total = cot_ref[:, to].astype(f32) + rows[:, at] + more[j * tok : (j + 1) * tok]
            out_ref[:, to] = total.astype(bf16)


def finish(spot, cotang, backs):
    width = cotang.shape[1]
    return pl.pallas_call(
        functools.partial(finish_kernel, ((0, P_SPLIT), (P_SPLIT, width - P_SPLIT))),
        out_shape=jax.ShapeDtypeStruct(cotang.shape, bf16),
        compiler_params=params(),
        cost_estimate=pl.CostEstimate(flops=10**9, bytes_accessed=4 * 2**20, transcendentals=0),
    )(spot, cotang, *backs)


def on_device(saved_inputs, out_cotangent, router, w_gate, w_up, w_down, expert_ids):
    inputs, cotang, router_t = saved_inputs[0], out_cotangent[0], router[0].T
    gate_w, up_w, down_w = w_gate[0, 0], w_up[0, 0], w_down[0, 0]
    experts = lax.axis_size("expert")
    n_group = lax.axis_size("tensor")
    tok, width = inputs.shape
    n_main = experts * MAIN
    pieces = MAIN // EXTRA
    rows = experts * (MAIN + EXTRA)
    ff = gate_w.shape[1]

    send, spot, raw = send_slots(expert_ids[0].T, inputs, cotang, experts, pieces)
    got = exchanged(send.reshape(experts, MAIN, -1)).reshape(n_main, -1)
    raws = gathered_x(raw)
    wide = wide_slots(raws, n_group, experts, pieces)
    got_wide = exchanged(wide)

    mine = (jnp.arange(experts, dtype=i32) == lax.axis_index("expert")).astype(f32)[None, :]
    s = jax.ShapeDtypeStruct
    shapes = (
        s((n_group, rows, width), bf16),
        s((n_group, rows, G_SLOT_COLS), bf16),
        s((n_group, rows, ff), f32),
        s((n_group, rows, ff), f32),
        s((n_group, rows, 2 * experts), f32),
    )
    half = n_main // 2
    above_lo, below_hi = along_x(got[:half], -1), along_x(got[half:], 1)
    above_hi, below_lo = along_x(got[half:], -1), along_x(got[:half], 1)
    weights = (gate_w, up_w, router_t, mine)
    slots = slot_rows((got,), weights, shapes, 0, (), pieces)
    slots, above_hi, below_lo = lax.optimization_barrier((slots, above_hi, below_lo))
    far1, far2 = along_x(above_lo, -1), along_x(below_hi, 1)
    slots = slot_rows((above_lo, above_hi), weights, shapes, 1, slots, pieces)
    slots = slot_rows((below_lo, below_hi), weights, shapes, 3, slots, pieces)
    x_rows, g_act, d_all, *part_a = owner_back(
        slots, (far1, far2), got_wide, (gate_w, up_w, down_w, router_t, mine), n_group, pieces, pieces
    )
    part_b = rest_back(d_all, gate_w, up_w, router_t)

    own, far_lo, far_hi, up_lo, up_hi, down_lo, down_hi = part_a
    first_a = ring_first(far_lo, far_hi, up_hi, down_lo)
    part_b, first_a = lax.optimization_barrier((part_b, first_a))
    sums_a = ring_second(own, up_lo, down_hi, *first_a)
    back_a = exchanged(sums_a.reshape(experts, MAIN, -1)).reshape(n_main, -1)
    own, far_lo, far_hi, up_lo, up_hi, down_lo, down_hi = part_b
    first_b = ring_first(far_lo, far_hi, up_hi, down_lo)
    x_rows, d_all, _ = lax.optimization_barrier((x_rows, d_all, sums_a))
    grad_gate, grad_up, router_part = x_gradients(x_rows, d_all, ff, experts)
    first_b, router_part = lax.optimization_barrier((first_b, router_part))
    router_part = ring_total(router_part, along_z)
    g_act, _, _ = lax.optimization_barrier((g_act, first_b, back_a))
    grad_down = down_gradient(width, slots[1], (far1, far2), got_wide, g_act, pieces, pieces)
    sums_b = ring_second(own, up_lo, down_hi, *first_b)
    sums_b, back_a, grad_down, router_part = lax.optimization_barrier((sums_b, back_a, grad_down, router_part))
    back_b = exchanged(sums_b.reshape(experts, MAIN, -1)).reshape(n_main, -1)
    backs = [back_a, back_b]
    router_total = ring_total(ring_total(router_part, along_y), along_x)

    cot_out = finish(spot, cotang, backs)
    n_sec = lax.axis_size("section")
    passed = lax.ppermute(cot_out, "section", [((i + 1) % n_sec, i) for i in range(n_sec)])
    return (
        passed[None],
        router_total.T[None],
        grad_gate[None, None],
        grad_up[None, None],
        grad_down[None, None],
    )


def solution(mesh):
    return jax.shard_map(
        on_device,
        mesh=mesh,
        in_specs=(
            P("section", ("expert", "tensor"), None),
            P("section", ("expert", "tensor"), None),
            P("section", None, None),
            P("section", "expert", None, "tensor"),
            P("section", "expert", None, "tensor"),
            P("section", "expert", "tensor", None),
            P("section", ("expert", "tensor"), None),
        ),
        out_specs=(
            P("section", ("expert", "tensor"), None),
            P("section", None, None),
            P("section", "expert", None, "tensor"),
            P("section", "expert", None, "tensor"),
            P("section", "expert", "tensor", None),
        ),
        check_vma=False,
    )
```

```python
import functools

import jax
import jax.numpy as jnp
from jax import lax
from jax.experimental import pallas as pl
from jax.experimental.pallas import tpu as pltpu
from jax.sharding import PartitionSpec as P

routed_scale = 16.0
MAIN = 16
EXTRA = 2
G_SLOT_COLS = 512
P_SPLIT = 1024
STEP = 512
VMEM_BYTES = 60 * 2**20
SMALL_VMEM = 28 * 2**20
bf16 = jnp.bfloat16
f32 = jnp.float32
i32 = jnp.int32


def along_x(block, step):
    n = lax.axis_size("tensor")
    return lax.ppermute(block, "tensor", [(i, (i + step) % n) for i in range(n)])


def along_plane(block, step_y, step_z):
    n = lax.axis_size("expert")
    side = int(round(n**0.5))
    route = [
        (y * side + z, (y + step_y) % side * side + (z + step_z) % side)
        for y in range(side)
        for z in range(side)
    ]
    return lax.ppermute(block, "expert", route)


def gathered_x(block):
    half = block.shape[0] // 2
    lo, hi = block[:half], block[half:]
    above_lo, below_hi = along_x(lo, -1), along_x(hi, 1)
    above_hi, below_lo = along_x(hi, -1), along_x(lo, 1)
    return above_lo, above_hi, along_x(above_lo, -1), along_x(below_hi, 1), below_lo, below_hi


def add(a, b):
    return (a.astype(f32) + b.astype(f32)).astype(bf16)


def ring_first(far_lo, far_hi, up_hi, down_lo):
    return along_x(far_lo, 1), along_x(far_hi, -1), along_x(up_hi, 1), along_x(down_lo, -1)


def ring_second(own, up_lo, down_hi, from_below, from_above, hi_below, lo_above):
    half = up_lo.shape[0]
    lo_below = along_x(add(up_lo, from_below), 1)
    hi_above = along_x(add(down_hi, from_above), -1)
    lo = own[:half].astype(f32) + lo_below.astype(f32) + lo_above.astype(f32)
    hi = own[half:].astype(f32) + hi_below.astype(f32) + hi_above.astype(f32)
    return jnp.concatenate([lo.astype(bf16), hi.astype(bf16)], axis=0)


def along_y(block, step):
    return along_plane(block, step, 0)


def along_z(block, step):
    return along_plane(block, 0, step)


def ring_total(block, shift):
    return block + shift(block, 1) + shift(block, 2) + shift(block, 3)


def exchanged(block):
    return lax.all_to_all(block, "expert", split_axis=0, concat_axis=0, tiled=True)


def dot(a, b, contract=((1,), (0,))):
    return lax.dot_general(a, b, (contract, ((), ())), preferred_element_type=f32)


def iota(shape, dim):
    return lax.broadcasted_iota(i32, shape, dim)


def spread_spots(spot):
    experts, tok = spot.shape
    n = experts * MAIN
    return jnp.broadcast_to(spot[:, None, :], (experts, MAIN, tok)).reshape(n, tok).astype(i32)


def put_slot(spots):
    return (spots == iota(spots.shape, 0) % MAIN).astype(bf16)


def put_folded(spots, j):
    slot = iota(spots.shape, 0) % MAIN
    return ((spots == MAIN + slot - j * EXTRA) & (slot // EXTRA == j)).astype(bf16)


def place(spots, payload, pieces):
    piece = payload.shape[1] // pieces
    total = jnp.zeros((spots.shape[0], piece), f32)
    for j in range(pieces):
        total = total + dot(put_folded(spots, j), payload[:, j * piece : (j + 1) * piece])
    return dot(put_slot(spots), payload).astype(bf16), total.astype(bf16)


def unfold(packed, pieces):
    n = packed.shape[0]
    rest = n // MAIN * EXTRA
    a = iota((pieces * rest, n), 0)
    source = a % rest // EXTRA * MAIN + a // rest * EXTRA + a % EXTRA
    spread = dot((source == iota((pieces * rest, n), 1)).astype(bf16), packed).astype(bf16)
    return jnp.concatenate([spread[j * rest : (j + 1) * rest] for j in range(pieces)], axis=1)


def fold(pieces, n):
    rest = n // MAIN * EXTRA
    a = iota((n, len(pieces) * rest), 1)
    goes = a % rest // EXTRA * MAIN + a // rest * EXTRA + a % EXTRA
    pack = (iota((n, len(pieces) * rest), 0) == goes).astype(bf16)
    return dot(pack, jnp.concatenate(pieces, axis=0)).astype(bf16)


def whole(a):
    return pl.BlockSpec(a.shape, lambda *i: (0,) * a.ndim)


def params(size=VMEM_BYTES):
    return pltpu.CompilerParams(vmem_limit_bytes=size)


def send_kernel(g_cols, pieces, ids_ref, x_ref, g_ref, out_ref, spot_ref, raw_ref):
    experts, tok = spot_ref.shape
    width = x_ref.shape[1] + g_cols
    e = iota((experts, tok), 0)
    hot = (ids_ref[0:1] == e) | (ids_ref[1:2] == e)
    earlier = (iota((tok, tok), 0) < iota((tok, tok), 1)).astype(bf16)
    spot = jnp.where(hot, dot(hot.astype(bf16), earlier), -1.0)
    spot_ref[...] = spot.astype(bf16)
    raw_ref[:, : raw_ref.shape[1] - tok] = g_ref[:, g_cols:]
    raw_ref[:, raw_ref.shape[1] - tok :] = jnp.concatenate([spot, jnp.zeros((tok - experts, tok), f32)], axis=0).T.astype(
        bf16
    )
    payload = jnp.concatenate([x_ref[...], g_ref[:, :g_cols]], axis=1)
    out_ref[:, :width], out_ref[:, width:] = place(spread_spots(spot), payload, pieces)


def send_slots(ids, x, g, experts, pieces):
    tok, width = x.shape[0], x.shape[1] + G_SLOT_COLS
    n = experts * MAIN
    s = jax.ShapeDtypeStruct
    return pl.pallas_call(
        functools.partial(send_kernel, G_SLOT_COLS, pieces),
        out_shape=(
            s((n, width + width // pieces), bf16),
            s((experts, tok), bf16),
            s((tok, g.shape[1] - G_SLOT_COLS + tok), bf16),
        ),
        compiler_params=params(),
        cost_estimate=pl.CostEstimate(flops=2 * n * tok * width * 2, bytes_accessed=4 * 2**20, transcendentals=0),
    )(ids, x, g)


def wide_kernel(pieces, own_ref, *refs):
    out_ref, held, sems = refs[6:]
    experts = out_ref.shape[0]
    tok = own_ref.shape[0]
    width = own_ref.shape[1] - tok
    pairs = [jnp.concatenate([refs[k][...], refs[k + 1][...]], axis=0) for k in (0, 2, 4)]
    copies = []
    for r, raw in enumerate((own_ref[...], *pairs)):
        at = slice(r * MAIN, (r + 1) * MAIN)
        spot = raw[:, width:].astype(f32).T[:experts]
        main, folded = place(spread_spots(spot), raw[:, :width], pieces)
        held[:, at, :width] = main.reshape(experts, MAIN, width)
        held[:, at, width:] = folded.reshape(experts, MAIN, width // pieces)
        copies.append(pltpu.make_async_copy(held.at[:, at], out_ref.at[:, at], sems.at[r]))
        copies[-1].start()
    for c in copies:
        c.wait()


def wide_slots(raws, n_group, experts, pieces):
    tok = raws[0].shape[0]
    width = raws[0].shape[1] - tok
    shape = (experts, n_group * MAIN, width + width // pieces)
    return pl.pallas_call(
        functools.partial(wide_kernel, pieces),
        out_shape=jax.ShapeDtypeStruct(shape, bf16),
        out_specs=pl.BlockSpec(memory_space=pltpu.HBM),
        scratch_shapes=[pltpu.VMEM(shape, bf16), pltpu.SemaphoreType.DMA((n_group,))],
        compiler_params=params(SMALL_VMEM),
        cost_estimate=pl.CostEstimate(
            flops=2 * experts * MAIN * n_group * tok * width * 2, bytes_accessed=8 * 2**20, transcendentals=0
        ),
    )(*raws)


def lay_out(parts, width, full, pieces, x_ref, g_ref):
    n = sum(p.shape[0] for p in parts)
    at = 0
    for p in parts:
        m = p.shape[0]
        x_ref[0, at : at + m] = p[:, :width]
        g_ref[0, at : at + m] = p[:, width:full]
        at += m
    extra = unfold(jnp.concatenate([p[:, full:] for p in parts], axis=0), pieces)
    x_ref[0, n:] = extra[:, :width]
    g_ref[0, n:] = extra[:, width:]


def x_part(x, w_refs, router_ref, mine_ref, h_ref, u_ref, aux_ref):
    experts = router_ref.shape[0]
    ff = h_ref.shape[2]
    both = jnp.concatenate([dot(x, w[...]) for w in w_refs], axis=1)
    h_ref[0] = both[:, :ff]
    u_ref[0] = both[:, ff:]
    exp_logit = jnp.exp(dot(x, router_ref[...], ((1,), (1,))))
    prob = exp_logit / jnp.sum(exp_logit, axis=1, keepdims=True)
    gate = jnp.sum(prob * mine_ref[...], axis=1, keepdims=True)
    base = routed_scale * prob * (mine_ref[...] - gate)
    scale = routed_scale * gate.astype(bf16).astype(f32)
    aux_ref[0] = jnp.concatenate([base, jnp.broadcast_to(scale, base.shape)], axis=1)


def rows_kernel(g_cols, pieces, n_parts, *refs):
    gate_ref, up_ref, router_ref, mine_ref = refs[n_parts : n_parts + 4]
    x_ref, g_ref, h_ref, u_ref, aux_ref = refs[-5:]
    width = x_ref.shape[2]
    lay_out(refs[:n_parts], width, width + g_cols, pieces, x_ref, g_ref)
    x_part(x_ref[0], (gate_ref, up_ref), router_ref, mine_ref, h_ref, u_ref, aux_ref)


def slot_rows(parts, weights, shapes, at, before, pieces):
    def block(s):
        return pl.BlockSpec((1, *s.shape[1:]), lambda i: (at, 0, 0))

    rows, width = shapes[0].shape[1:]
    args = (*parts, *weights)
    return pl.pallas_call(
        functools.partial(rows_kernel, G_SLOT_COLS, pieces, len(parts)),
        grid=(1,),
        out_shape=shapes,
        in_specs=[whole(a) for a in args] + [pl.BlockSpec(memory_space=pl.ANY)] * len(before),
        out_specs=[block(s) for s in shapes],
        input_output_aliases={len(args) + i: i for i in range(len(before))},
        compiler_params=params(),
        cost_estimate=pl.CostEstimate(
            flops=2 * rows * width * 1024, bytes_accessed=10 * 2**20, transcendentals=rows * 16
        ),
    )(*args, *before)


def turned(w_back, w_in, router):
    ff2 = w_in.shape[1]
    w_back[:ff2] = w_in.T
    pad = jnp.zeros((w_back.shape[0] - ff2 - router.shape[0], router.shape[1]), bf16)
    w_back[ff2:] = jnp.concatenate([router, pad], axis=0)


def send_back(d, w_back, pa, out_refs, sems):
    n_group, n, total = pa.shape
    cols = w_back.shape[1]
    piece = total - cols
    rows = d.shape[0] // n_group
    half = n // 2
    lo, hi = slice(0, half), slice(half, n)
    parts = ((0, slice(0, n)), (2, lo), (2, hi), (1, lo), (1, hi), (3, lo), (3, hi))
    out = []

    def send(at, k):
        for j, ((q, part), to) in enumerate(zip(parts, out_refs)):
            out.append(pltpu.make_async_copy(pa.at[q, part, at], to.at[:, at], sems.at[k, j]))
            out[-1].start()

    extra = [[] for _ in range(n_group)]
    for k, c in enumerate(range(0, cols, STEP)):
        at = slice(c, c + STEP)
        p = dot(d, w_back[:, at]).astype(bf16)
        for q in range(n_group):
            pa[q, :, at] = p[q * rows : q * rows + n]
            extra[q] += [p[q * rows + n : (q + 1) * rows, j : j + piece] for j in range(0, STEP, piece)]
        send(at, k)
    for q in range(n_group):
        pa[q, :, cols:] = fold(extra[q], n)
    send(slice(cols, total), cols // STEP)
    for c in out:
        c.wait()


def back_shapes(n, cols, piece):
    s = jax.ShapeDtypeStruct
    return (s((n, cols + piece), bf16),) + (s((n // 2, cols + piece), bf16),) * 6


def piece_of(cols):
    return -(-cols // (MAIN // EXTRA * 128)) * 128


def whole_rows(g, slot_cols, wide_ref, pieces):
    first = slot_cols.shape[1]
    n = wide_ref.shape[0] * MAIN
    wide = g.shape[1] - first
    g[:, :first] = slot_cols
    g[:n, first:] = wide_ref[:, :, :wide].reshape(n, wide)
    g[n:, first:] = unfold(wide_ref[:, :, wide:].reshape(n, wide // pieces), pieces)


def back_kernel(n_group, x_pieces, wide_pieces, *refs):
    (gs_ref, wide_ref, h_ref, u_ref, aux_ref, router_ref, mine_ref) = refs[:7]
    from_refs = refs[7:12]
    x_out, ga_ref, d_out = refs[13:16]
    out_refs = refs[16:23]
    x, d_ref, g, hs, us, axs, gs, down_ref, w_in_ref, far1_ref, far2_ref, w_back, pa, in_sems, a_sems, out_sems = refs[23:]
    i = pl.program_id(0)
    last = n_group - 1
    r = i + (i == 2).astype(i32) - (i == 3).astype(i32)
    experts = wide_ref.shape[0]
    n = experts * MAIN
    first = gs_ref.shape[2]
    width = g.shape[1]
    ff = h_ref.shape[2]
    rows = h_ref.shape[1]
    cols = w_back.shape[1]
    lands = (down_ref, w_in_ref.at[:, :ff], w_in_ref.at[:, ff:], far1_ref, far2_ref)
    copies = [pltpu.make_async_copy(s, d, in_sems.at[k]) for k, (s, d) in enumerate(zip(from_refs, lands))]

    x_leaves = pltpu.make_async_copy(x, x_out.at[pl.ds(2, 1)], out_sems.at[n_group])
    d_leaves = [pltpu.make_async_copy(d_ref.at[q], d_out.at[q], out_sems.at[q]) for q in range(n_group)]

    @pl.when(i == 0)
    def _():
        for c in copies:
            c.start()
        copies[0].wait()

    @pl.when(i < last)
    def _():
        hs[...], us[...], axs[...], gs[...] = h_ref[...], u_ref[...], aux_ref[...], gs_ref[...]

    @pl.when(i == last)
    def _():
        copies[3].wait()
        copies[4].wait()
        lay_out((far1_ref, far2_ref), width, width + first, x_pieces, x, gs)
        x_leaves.start()
        x_part(x[0], (w_in_ref,), router_ref, mine_ref, hs, us, axs)

    whole_rows(g, gs[0], wide_ref, wide_pieces)
    e = dot(g[...], down_ref[...], ((1,), (1,)))
    hidden, up_value = hs[0], us[0]
    base, scaled = axs[0, :, :experts], axs[0, :, experts : experts + 1]
    sig = 1.0 / (1.0 + jnp.exp(-hidden))
    silu = hidden * sig
    product = silu * up_value
    part = jnp.sum(product * e, axis=1, keepdims=True)
    grad = scaled * e
    dh = (grad * up_value * (sig * (1.0 + hidden * (1.0 - sig)))).astype(bf16)
    du = (grad * silu).astype(bf16)
    dl = (part * base).astype(bf16)
    pad = jnp.zeros((rows, d_ref.shape[2] - 2 * ff - experts), bf16)
    d_ref[r] = jnp.concatenate([dh, du, dl, pad], axis=1)
    ga_ref[0] = (scaled * product).astype(bf16)

    for q in range(n_group):

        @pl.when(r == q)
        def _():
            d_leaves[q].start()

    @pl.when(i == 1)
    def _():
        copies[1].wait()
        copies[2].wait()
        turned(w_back, w_in_ref[:cols], router_ref[:, :cols])

    @pl.when(i == last)
    def _():
        d = d_ref[...].reshape(n_group * rows, d_ref.shape[2])
        send_back(d, w_back, pa, out_refs, a_sems)
        for c in (x_leaves, *d_leaves):
            c.wait()


def owner_back(slots, far, wide, weights, n_group, pieces, wide_pieces):
    x, gs, h, u, aux = slots
    gate_w, up_w, down_w, router_t, mine = weights
    rows, ff = h.shape[1:]
    width = x.shape[2]
    experts = wide.shape[0]
    n = experts * MAIN
    piece = piece_of(P_SPLIT)

    def turn(i):
        return i + (i == 2).astype(i32) - (i == 3).astype(i32)

    def block(a):
        return pl.BlockSpec((1, *a.shape[1:]), lambda i: (turn(i), 0, 0))

    s = jax.ShapeDtypeStruct
    out = (
        s(x.shape, bf16),
        s((n_group, rows, ff), bf16),
        s((n_group, rows, 2 * ff + 128), bf16),
        *back_shapes(n, P_SPLIT, piece),
    )
    later = (down_w, gate_w, up_w, *far)
    here = pl.BlockSpec(memory_space=pl.ANY)
    return pl.pallas_call(
        functools.partial(back_kernel, n_group, pieces, wide_pieces),
        grid=(n_group,),
        out_shape=out,
        in_specs=[
            block(gs),
            pl.BlockSpec((experts, MAIN, wide.shape[2]), lambda i: (0, turn(i), 0)),
            block(h),
            block(u),
            block(aux),
            whole(router_t),
            whole(mine),
        ]
        + [here] * (len(later) + 1),
        out_specs=[here, block(out[1]), here]
        + [here] * 7,
        scratch_shapes=[
            pltpu.VMEM((1, rows, width), bf16),
            pltpu.VMEM(out[2].shape, bf16),
            pltpu.VMEM((rows, width), bf16),
            pltpu.VMEM((1, rows, ff), f32),
            pltpu.VMEM((1, rows, ff), f32),
            pltpu.VMEM((1, *aux.shape[1:]), f32),
            pltpu.VMEM((1, rows, gs.shape[2]), bf16),
            pltpu.VMEM(down_w.shape, bf16),
            pltpu.VMEM((width, 2 * ff), bf16),
            pltpu.VMEM(far[0].shape, bf16),
            pltpu.VMEM(far[1].shape, bf16),
            pltpu.VMEM((2 * ff + 128, P_SPLIT), bf16),
            pltpu.VMEM((n_group, n, P_SPLIT + piece), bf16),
            pltpu.SemaphoreType.DMA((len(later),)),
            pltpu.SemaphoreType.DMA((P_SPLIT // STEP + 1, 7)),
            pltpu.SemaphoreType.DMA((n_group + 1,)),
        ],
        input_output_aliases={12: 0},
        compiler_params=params(),
        cost_estimate=pl.CostEstimate(
            flops=6 * n_group * rows * width * ff, bytes_accessed=40 * 2**20, transcendentals=n_group * rows * ff
        ),
    )(gs, wide, h, u, aux, router_t, mine, *later, x)


def down_kernel(x_pieces, wide_pieces, gs_ref, wide_ref, ga_ref, far1_ref, far2_ref, out_ref, x, gs, g):
    r = pl.program_id(0)
    first = gs_ref.shape[2]
    n_group, rows, ff = ga_ref.shape
    width = g.shape[2]

    @pl.when(r == 2)
    def _():
        lay_out((far1_ref, far2_ref), width, width + first, x_pieces, x, gs)

    @pl.when(r != 2)
    def _():
        gs[...] = gs_ref[...]

    whole_rows(g.at[r], gs[0], wide_ref, wide_pieces)

    @pl.when(r == n_group - 1)
    def _():
        turned_act = ga_ref[...].reshape(n_group * rows, ff).T
        for c in range(0, width, STEP):
            at = slice(c, c + STEP)
            out_ref[:, at] = dot(turned_act, g[:, :, at].reshape(n_group * rows, STEP)).astype(bf16)


def down_gradient(width, gs, far, wide, g_act, pieces, wide_pieces):
    n_group, rows, ff = g_act.shape
    experts = wide.shape[0]
    out = jax.ShapeDtypeStruct((ff, width), bf16)
    return pl.pallas_call(
        functools.partial(down_kernel, pieces, wide_pieces),
        grid=(n_group,),
        out_shape=out,
        in_specs=[
            pl.BlockSpec((1, *gs.shape[1:]), lambda i: (i, 0, 0)),
            pl.BlockSpec((experts, MAIN, wide.shape[2]), lambda i: (0, i, 0)),
            whole(g_act),
            whole(far[0]),
            whole(far[1]),
        ],
        out_specs=whole(out),
        scratch_shapes=[
            pltpu.VMEM((1, rows, width), bf16),
            pltpu.VMEM((1, rows, gs.shape[2]), bf16),
            pltpu.VMEM((n_group, rows, width), bf16),
        ],
        compiler_params=params(),
        cost_estimate=pl.CostEstimate(
            flops=2 * n_group * rows * width * ff, bytes_accessed=16 * 2**20, transcendentals=0
        ),
    )(gs, wide, g_act, *far)


def x_kernel(experts, x_ref, d_ref, gate_ref, up_ref, router_ref):
    ff = gate_ref.shape[1]
    rows = x_ref.shape[0] * x_ref.shape[1]
    x = x_ref[...].reshape(rows, x_ref.shape[2])
    d = d_ref[...].reshape(rows, d_ref.shape[2])
    both = dot(x.T, d[:, : 2 * ff])
    gate_ref[...] = both[:, :ff].astype(bf16)
    up_ref[...] = both[:, ff:].astype(bf16)
    router_ref[...] = dot(d[:, 2 * ff :], x, ((0,), (0,)))[:experts]


def x_gradients(x_rows, d, ff, experts):
    n_group, rows, width = x_rows.shape
    s = jax.ShapeDtypeStruct
    return pl.pallas_call(
        functools.partial(x_kernel, experts),
        grid=(width // STEP,),
        out_shape=(s((width, ff), bf16), s((width, ff), bf16), s((experts, width), f32)),
        in_specs=[pl.BlockSpec((n_group, rows, STEP), lambda c: (0, 0, c)), whole(d)],
        out_specs=[
            pl.BlockSpec((STEP, ff), lambda c: (c, 0)),
            pl.BlockSpec((STEP, ff), lambda c: (c, 0)),
            pl.BlockSpec((experts, STEP), lambda c: (0, c)),
        ],
        compiler_params=params(SMALL_VMEM),
        cost_estimate=pl.CostEstimate(
            flops=4 * n_group * rows * width * ff, bytes_accessed=12 * 2**20, transcendentals=0
        ),
    )(x_rows, d)


def rest_back_kernel(d_ref, gate_ref, up_ref, router_ref, *refs):
    out_refs = refs[:7]
    w_in, w_back, pa, in_sems, sems = refs[7:]
    n_group, rows = d_ref.shape[:2]
    ff = gate_ref.shape[1]
    cols = w_back.shape[1]
    first = gate_ref.shape[0] - cols
    copies = [
        pltpu.make_async_copy(w.at[pl.ds(first, cols)], w_in.at[:, k * ff : (k + 1) * ff], in_sems.at[k])
        for k, w in enumerate((gate_ref, up_ref))
    ]
    for c in copies:
        c.start()
    for c in copies:
        c.wait()
    turned(w_back, w_in[...], router_ref[:, first:])
    send_back(d_ref[...].reshape(n_group * rows, d_ref.shape[2]), w_back, pa, out_refs, sems)


def rest_back(d, gate_w, up_w, router_t):
    n_group, rows = d.shape[:2]
    width, ff = gate_w.shape
    n = router_t.shape[0] * MAIN
    cols = width - P_SPLIT
    piece = piece_of(cols)
    here = pl.BlockSpec(memory_space=pl.ANY)
    return pl.pallas_call(
        rest_back_kernel,
        out_shape=back_shapes(n, cols, piece),
        in_specs=[pl.BlockSpec(memory_space=pltpu.VMEM), here, here, pl.BlockSpec(memory_space=pltpu.VMEM)],
        out_specs=[here] * 7,
        scratch_shapes=[
            pltpu.VMEM((cols, 2 * ff), bf16),
            pltpu.VMEM((2 * ff + 128, cols), bf16),
            pltpu.VMEM((n_group, n, cols + piece), bf16),
            pltpu.SemaphoreType.DMA((2,)),
            pltpu.SemaphoreType.DMA((cols // STEP + 1, 7)),
        ],
        compiler_params=params(SMALL_VMEM),
        cost_estimate=pl.CostEstimate(
            flops=4 * n_group * rows * ff * cols, bytes_accessed=12 * 2**20, transcendentals=0
        ),
    )(d, gate_w, up_w, router_t)


def finish_kernel(splits, spot_ref, cot_ref, *refs):
    out_ref = refs[-1]
    tok = cot_ref.shape[0]
    spots = spread_spots(spot_ref[...].astype(f32))
    main = put_slot(spots)
    folded = [put_folded(spots, j) for j in range(MAIN // EXTRA)]
    for (first, cols), back_ref in zip(splits, refs[:-1]):
        q = back_ref.shape[1] - cols
        pieces = cols // q
        rows = dot(main, back_ref[:, :cols], ((0,), (0,)))
        more = dot(jnp.concatenate(folded[:pieces], axis=1), back_ref[:, cols:], ((0,), (0,)))
        for j in range(pieces):
            at = slice(j * q, (j + 1) * q)
            to = slice(first + j * q, first + (j + 1) * q)
            total = cot_ref[:, to].astype(f32) + rows[:, at] + more[j * tok : (j + 1) * tok]
            out_ref[:, to] = total.astype(bf16)


def finish(spot, cotang, backs):
    width = cotang.shape[1]
    return pl.pallas_call(
        functools.partial(finish_kernel, ((0, P_SPLIT), (P_SPLIT, width - P_SPLIT))),
        out_shape=jax.ShapeDtypeStruct(cotang.shape, bf16),
        compiler_params=params(SMALL_VMEM),
        cost_estimate=pl.CostEstimate(flops=10**9, bytes_accessed=4 * 2**20, transcendentals=0),
    )(spot, cotang, *backs)


def on_device(saved_inputs, out_cotangent, router, w_gate, w_up, w_down, expert_ids):
    inputs, cotang, router_t = saved_inputs[0], out_cotangent[0], router[0].T
    gate_w, up_w, down_w = w_gate[0, 0], w_up[0, 0], w_down[0, 0]
    experts = lax.axis_size("expert")
    n_group = lax.axis_size("tensor")
    tok, width = inputs.shape
    n_main = experts * MAIN
    pieces = MAIN // EXTRA
    rows = experts * (MAIN + EXTRA)
    ff = gate_w.shape[1]

    send, spot, raw = send_slots(expert_ids[0].T, inputs, cotang, experts, pieces)
    got = exchanged(send.reshape(experts, MAIN, -1)).reshape(n_main, -1)
    wide = wide_slots((raw, *gathered_x(raw)), n_group, experts, pieces)
    got_wide = exchanged(wide)

    mine = (jnp.arange(experts, dtype=i32) == lax.axis_index("expert")).astype(f32)[None, :]
    s = jax.ShapeDtypeStruct
    shapes = (
        s((n_group, rows, width), bf16),
        s((n_group, rows, G_SLOT_COLS), bf16),
        s((n_group, rows, ff), f32),
        s((n_group, rows, ff), f32),
        s((n_group, rows, 2 * experts), f32),
    )
    above_lo, above_hi, far1, far2, below_lo, below_hi = gathered_x(got)
    weights = (gate_w, up_w, router_t, mine)
    slots = slot_rows((got,), weights, shapes, 0, (), pieces)
    slots, above_hi, below_lo = lax.optimization_barrier((slots, above_hi, below_lo))
    slots = slot_rows((above_lo, above_hi), weights, shapes, 1, slots, pieces)
    slots = slot_rows((below_lo, below_hi), weights, shapes, 3, slots, pieces)
    x_rows, g_act, d_all, *part_a = owner_back(
        slots, (far1, far2), got_wide, (gate_w, up_w, down_w, router_t, mine), n_group, pieces, pieces
    )
    part_b = rest_back(d_all, gate_w, up_w, router_t)

    own, far_lo, far_hi, up_lo, up_hi, down_lo, down_hi = part_a
    first_a = ring_first(far_lo, far_hi, up_hi, down_lo)
    x_rows, d_all, first_a = lax.optimization_barrier((x_rows, d_all, first_a))
    grad_gate, grad_up, router_part = x_gradients(x_rows, d_all, ff, experts)
    part_b, router_part = lax.optimization_barrier((part_b, router_part))
    sums_a = ring_second(own, up_lo, down_hi, *first_a)
    back_a = exchanged(sums_a.reshape(experts, MAIN, -1)).reshape(n_main, -1)
    own, far_lo, far_hi, up_lo, up_hi, down_lo, down_hi = part_b
    first_b = ring_first(far_lo, far_hi, up_hi, down_lo)
    router_part, back_a = lax.optimization_barrier((router_part, back_a))
    router_part = ring_total(router_part, along_z)
    g_act, _, _ = lax.optimization_barrier((g_act, first_b, back_a))
    grad_down = down_gradient(width, slots[1], (far1, far2), got_wide, g_act, pieces, pieces)
    sums_b = ring_second(own, up_lo, down_hi, *first_b)
    sums_b, router_part = lax.optimization_barrier((sums_b, router_part))
    back_b = exchanged(sums_b.reshape(experts, MAIN, -1)).reshape(n_main, -1)
    back_b, grad_down = lax.optimization_barrier((back_b, grad_down))
    router_total = ring_total(ring_total(router_part, along_y), along_x)

    cot_out = finish(spot, cotang, (back_a, back_b))
    n_sec = lax.axis_size("section")
    passed = lax.ppermute(cot_out, "section", [((i + 1) % n_sec, i) for i in range(n_sec)])
    return (
        passed[None],
        router_total.T[None],
        grad_gate[None, None],
        grad_up[None, None],
        grad_down[None, None],
    )


def solution(mesh):
    return jax.shard_map(
        on_device,
        mesh=mesh,
        in_specs=(
            P("section", ("expert", "tensor"), None),
            P("section", ("expert", "tensor"), None),
            P("section", None, None),
            P("section", "expert", None, "tensor"),
            P("section", "expert", None, "tensor"),
            P("section", "expert", "tensor", None),
            P("section", ("expert", "tensor"), None),
        ),
        out_specs=(
            P("section", ("expert", "tensor"), None),
            P("section", None, None),
            P("section", "expert", None, "tensor"),
            P("section", "expert", None, "tensor"),
            P("section", "expert", "tensor", None),
        ),
        check_vma=False,
    )
```

```python
import functools

import jax
import jax.numpy as jnp
from jax import lax
from jax.experimental import pallas as pl
from jax.experimental.pallas import tpu as pltpu
from jax.sharding import PartitionSpec as P

routed_scale = 16.0
MAIN = 16
EXTRA = 2
G_SLOT_COLS = 512
P_SPLIT = 1024
STEP = 512
VMEM_BYTES = 60 * 2**20
SMALL_VMEM = 28 * 2**20
bf16 = jnp.bfloat16
f32 = jnp.float32
i32 = jnp.int32


def along_x(block, step):
    n = lax.axis_size("tensor")
    return lax.ppermute(block, "tensor", [(i, (i + step) % n) for i in range(n)])


def along_plane(block, step_y, step_z):
    n = lax.axis_size("expert")
    side = int(round(n**0.5))
    route = [
        (y * side + z, (y + step_y) % side * side + (z + step_z) % side)
        for y in range(side)
        for z in range(side)
    ]
    return lax.ppermute(block, "expert", route)


def gathered_x(block):
    half = block.shape[0] // 2
    lo, hi = block[:half], block[half:]
    above_lo, below_hi = along_x(lo, -1), along_x(hi, 1)
    above_hi, below_lo = along_x(hi, -1), along_x(lo, 1)
    return above_lo, above_hi, along_x(above_lo, -1), along_x(below_hi, 1), below_lo, below_hi


def add(a, b):
    return (a.astype(f32) + b.astype(f32)).astype(bf16)


def ring_first(far_lo, far_hi, up_hi, down_lo):
    return along_x(far_lo, 1), along_x(far_hi, -1), along_x(up_hi, 1), along_x(down_lo, -1)


def ring_second(own, up_lo, down_hi, from_below, from_above, hi_below, lo_above):
    half = up_lo.shape[0]
    lo_below = along_x(add(up_lo, from_below), 1)
    hi_above = along_x(add(down_hi, from_above), -1)
    lo = own[:half].astype(f32) + lo_below.astype(f32) + lo_above.astype(f32)
    hi = own[half:].astype(f32) + hi_below.astype(f32) + hi_above.astype(f32)
    return jnp.concatenate([lo.astype(bf16), hi.astype(bf16)], axis=0)


def along_y(block, step):
    return along_plane(block, step, 0)


def along_z(block, step):
    return along_plane(block, 0, step)


def ring_total(block, shift):
    return block + shift(block, 1) + shift(block, 2) + shift(block, 3)


def exchanged(block):
    return lax.all_to_all(block, "expert", split_axis=0, concat_axis=0, tiled=True)


def dot(a, b, contract=((1,), (0,))):
    return lax.dot_general(a, b, (contract, ((), ())), preferred_element_type=f32)


def iota(shape, dim):
    return lax.broadcasted_iota(i32, shape, dim)


def spread_spots(spot):
    experts, tok = spot.shape
    n = experts * MAIN
    return jnp.broadcast_to(spot[:, None, :], (experts, MAIN, tok)).reshape(n, tok).astype(i32)


def put_slot(spots):
    return (spots == iota(spots.shape, 0) % MAIN).astype(bf16)


def put_folded(spots, j):
    slot = iota(spots.shape, 0) % MAIN
    return ((spots == MAIN + slot - j * EXTRA) & (slot // EXTRA == j)).astype(bf16)


def place(spots, payload, pieces):
    piece = payload.shape[1] // pieces
    total = jnp.zeros((spots.shape[0], piece), f32)
    for j in range(pieces):
        total = total + dot(put_folded(spots, j), payload[:, j * piece : (j + 1) * piece])
    return dot(put_slot(spots), payload).astype(bf16), total.astype(bf16)


def unfold(packed, pieces):
    n = packed.shape[0]
    rest = n // MAIN * EXTRA
    a = iota((pieces * rest, n), 0)
    source = a % rest // EXTRA * MAIN + a // rest * EXTRA + a % EXTRA
    spread = dot((source == iota((pieces * rest, n), 1)).astype(bf16), packed).astype(bf16)
    return jnp.concatenate([spread[j * rest : (j + 1) * rest] for j in range(pieces)], axis=1)


def fold(pieces, n):
    rest = n // MAIN * EXTRA
    a = iota((n, len(pieces) * rest), 1)
    goes = a % rest // EXTRA * MAIN + a // rest * EXTRA + a % EXTRA
    pack = (iota((n, len(pieces) * rest), 0) == goes).astype(bf16)
    return dot(pack, jnp.concatenate(pieces, axis=0)).astype(bf16)


def whole(a):
    return pl.BlockSpec(a.shape, lambda *i: (0,) * a.ndim)


def params(size=VMEM_BYTES):
    return pltpu.CompilerParams(vmem_limit_bytes=size)


def send_kernel(g_cols, pieces, ids_ref, x_ref, g_ref, out_ref, spot_ref, raw_ref):
    experts, tok = spot_ref.shape
    width = x_ref.shape[1] + g_cols
    e = iota((experts, tok), 0)
    hot = (ids_ref[0:1] == e) | (ids_ref[1:2] == e)
    earlier = (iota((tok, tok), 0) < iota((tok, tok), 1)).astype(bf16)
    spot = jnp.where(hot, dot(hot.astype(bf16), earlier), -1.0)
    spot_ref[...] = spot.astype(bf16)
    raw_ref[:, : raw_ref.shape[1] - tok] = g_ref[:, g_cols:]
    raw_ref[:, raw_ref.shape[1] - tok :] = jnp.concatenate([spot, jnp.zeros((tok - experts, tok), f32)], axis=0).T.astype(
        bf16
    )
    payload = jnp.concatenate([x_ref[...], g_ref[:, :g_cols]], axis=1)
    out_ref[:, :width], out_ref[:, width:] = place(spread_spots(spot), payload, pieces)


def send_slots(ids, x, g, experts, pieces):
    tok, width = x.shape[0], x.shape[1] + G_SLOT_COLS
    n = experts * MAIN
    s = jax.ShapeDtypeStruct
    return pl.pallas_call(
        functools.partial(send_kernel, G_SLOT_COLS, pieces),
        out_shape=(
            s((n, width + width // pieces), bf16),
            s((experts, tok), bf16),
            s((tok, g.shape[1] - G_SLOT_COLS + tok), bf16),
        ),
        compiler_params=params(),
        cost_estimate=pl.CostEstimate(flops=2 * n * tok * width * 2, bytes_accessed=4 * 2**20, transcendentals=0),
    )(ids, x, g)


def wide_kernel(pieces, own_ref, *refs):
    out_ref, held, sems = refs[6:]
    experts = out_ref.shape[0]
    tok = own_ref.shape[0]
    width = own_ref.shape[1] - tok
    pairs = [jnp.concatenate([refs[k][...], refs[k + 1][...]], axis=0) for k in (0, 2, 4)]
    copies = []
    for r, raw in enumerate((own_ref[...], *pairs)):
        at = slice(r * MAIN, (r + 1) * MAIN)
        spot = raw[:, width:].astype(f32).T[:experts]
        main, folded = place(spread_spots(spot), raw[:, :width], pieces)
        held[:, at, :width] = main.reshape(experts, MAIN, width)
        held[:, at, width:] = folded.reshape(experts, MAIN, width // pieces)
        copies.append(pltpu.make_async_copy(held.at[:, at], out_ref.at[:, at], sems.at[r]))
        copies[-1].start()
    for c in copies:
        c.wait()


def wide_slots(raws, n_group, experts, pieces):
    tok = raws[0].shape[0]
    width = raws[0].shape[1] - tok
    shape = (experts, n_group * MAIN, width + width // pieces)
    return pl.pallas_call(
        functools.partial(wide_kernel, pieces),
        out_shape=jax.ShapeDtypeStruct(shape, bf16),
        out_specs=pl.BlockSpec(memory_space=pltpu.HBM),
        scratch_shapes=[pltpu.VMEM(shape, bf16), pltpu.SemaphoreType.DMA((n_group,))],
        compiler_params=params(SMALL_VMEM),
        cost_estimate=pl.CostEstimate(
            flops=2 * experts * MAIN * n_group * tok * width * 2, bytes_accessed=8 * 2**20, transcendentals=0
        ),
    )(*raws)


def lay_out(parts, width, full, pieces, x_ref, g_ref):
    n = sum(p.shape[0] for p in parts)
    at = 0
    for p in parts:
        m = p.shape[0]
        x_ref[0, at : at + m] = p[:, :width]
        g_ref[0, at : at + m] = p[:, width:full]
        at += m
    extra = unfold(jnp.concatenate([p[:, full:] for p in parts], axis=0), pieces)
    x_ref[0, n:] = extra[:, :width]
    g_ref[0, n:] = extra[:, width:]


def x_part(x, w_refs, router_ref, mine_ref, h_ref, u_ref, aux_ref):
    experts = router_ref.shape[0]
    ff = h_ref.shape[2]
    both = jnp.concatenate([dot(x, w[...]) for w in w_refs], axis=1)
    h_ref[0] = both[:, :ff]
    u_ref[0] = both[:, ff:]
    exp_logit = jnp.exp(dot(x, router_ref[...], ((1,), (1,))))
    prob = exp_logit / jnp.sum(exp_logit, axis=1, keepdims=True)
    gate = jnp.sum(prob * mine_ref[...], axis=1, keepdims=True)
    base = routed_scale * prob * (mine_ref[...] - gate)
    scale = routed_scale * gate.astype(bf16).astype(f32)
    aux_ref[0] = jnp.concatenate([base, jnp.broadcast_to(scale, base.shape)], axis=1)


def rows_kernel(g_cols, pieces, n_parts, *refs):
    gate_ref, up_ref, router_ref, mine_ref = refs[n_parts : n_parts + 4]
    x_ref, g_ref, h_ref, u_ref, aux_ref = refs[-5:]
    width = x_ref.shape[2]
    lay_out(refs[:n_parts], width, width + g_cols, pieces, x_ref, g_ref)
    x_part(x_ref[0], (gate_ref, up_ref), router_ref, mine_ref, h_ref, u_ref, aux_ref)


def slot_rows(parts, weights, shapes, at, before, pieces):
    def block(s):
        return pl.BlockSpec((1, *s.shape[1:]), lambda i: (at, 0, 0))

    rows, width = shapes[0].shape[1:]
    args = (*parts, *weights)
    return pl.pallas_call(
        functools.partial(rows_kernel, G_SLOT_COLS, pieces, len(parts)),
        grid=(1,),
        out_shape=shapes,
        in_specs=[whole(a) for a in args] + [pl.BlockSpec(memory_space=pl.ANY)] * len(before),
        out_specs=[block(s) for s in shapes],
        input_output_aliases={len(args) + i: i for i in range(len(before))},
        compiler_params=params(),
        cost_estimate=pl.CostEstimate(
            flops=2 * rows * width * 1024, bytes_accessed=10 * 2**20, transcendentals=rows * 16
        ),
    )(*args, *before)


def turned(w_back, w_in, router):
    ff2 = w_in.shape[1]
    w_back[:ff2] = w_in.T
    pad = jnp.zeros((w_back.shape[0] - ff2 - router.shape[0], router.shape[1]), bf16)
    w_back[ff2:] = jnp.concatenate([router, pad], axis=0)


def send_back(d, w_back, pa, out_refs, sems):
    n_group, n, total = pa.shape
    cols = w_back.shape[1]
    piece = total - cols
    rows = d.shape[0] // n_group
    half = n // 2
    lo, hi = slice(0, half), slice(half, n)
    parts = ((0, slice(0, n)), (2, lo), (2, hi), (1, lo), (1, hi), (3, lo), (3, hi))
    out = []

    def send(at, k):
        for j, ((q, part), to) in enumerate(zip(parts, out_refs)):
            out.append(pltpu.make_async_copy(pa.at[q, part, at], to.at[:, at], sems.at[k, j]))
            out[-1].start()

    extra = [[] for _ in range(n_group)]
    for k, c in enumerate(range(0, cols, STEP)):
        at = slice(c, c + STEP)
        p = dot(d, w_back[:, at]).astype(bf16)
        for q in range(n_group):
            pa[q, :, at] = p[q * rows : q * rows + n]
            extra[q] += [p[q * rows + n : (q + 1) * rows, j : j + piece] for j in range(0, STEP, piece)]
        send(at, k)
    for q in range(n_group):
        pa[q, :, cols:] = fold(extra[q], n)
    send(slice(cols, total), cols // STEP)
    for c in out:
        c.wait()


def back_shapes(n, cols, piece):
    s = jax.ShapeDtypeStruct
    return (s((n, cols + piece), bf16),) + (s((n // 2, cols + piece), bf16),) * 6


def piece_of(cols):
    return -(-cols // (MAIN // EXTRA * 128)) * 128


def whole_rows(g, slot_cols, wide_ref, pieces):
    first = slot_cols.shape[1]
    n = wide_ref.shape[0] * MAIN
    wide = g.shape[1] - first
    g[:, :first] = slot_cols
    g[:n, first:] = wide_ref[:, :, :wide].reshape(n, wide)
    g[n:, first:] = unfold(wide_ref[:, :, wide:].reshape(n, wide // pieces), pieces)


def back_kernel(n_group, x_pieces, wide_pieces, *refs):
    (gs_ref, wide_ref, h_ref, u_ref, aux_ref, router_ref, mine_ref) = refs[:7]
    from_refs = refs[7:12]
    x_out, ga_ref, d_out = refs[13:16]
    out_refs = refs[16:23]
    x, d_ref, g, hs, us, axs, gs, down_ref, w_in_ref, far1_ref, far2_ref, w_back, pa, in_sems, a_sems, out_sems = refs[23:]
    i = pl.program_id(0)
    last = n_group - 1
    r = i + (i == 2).astype(i32) - (i == 3).astype(i32)
    experts = wide_ref.shape[0]
    n = experts * MAIN
    first = gs_ref.shape[2]
    width = g.shape[1]
    ff = h_ref.shape[2]
    rows = h_ref.shape[1]
    cols = w_back.shape[1]
    lands = (down_ref, w_in_ref.at[:, :ff], w_in_ref.at[:, ff:], far1_ref, far2_ref)
    copies = [pltpu.make_async_copy(s, d, in_sems.at[k]) for k, (s, d) in enumerate(zip(from_refs, lands))]

    x_leaves = pltpu.make_async_copy(x, x_out.at[pl.ds(2, 1)], out_sems.at[n_group])
    d_leaves = [pltpu.make_async_copy(d_ref.at[q], d_out.at[q], out_sems.at[q]) for q in range(n_group)]

    @pl.when(i == 0)
    def _():
        for c in copies:
            c.start()
        copies[0].wait()

    @pl.when(i < last)
    def _():
        hs[...], us[...], axs[...], gs[...] = h_ref[...], u_ref[...], aux_ref[...], gs_ref[...]

    @pl.when(i == last)
    def _():
        copies[3].wait()
        copies[4].wait()
        lay_out((far1_ref, far2_ref), width, width + first, x_pieces, x, gs)
        x_leaves.start()
        x_part(x[0], (w_in_ref,), router_ref, mine_ref, hs, us, axs)

    whole_rows(g, gs[0], wide_ref, wide_pieces)
    e = dot(g[...], down_ref[...], ((1,), (1,)))
    hidden, up_value = hs[0], us[0]
    base, scaled = axs[0, :, :experts], axs[0, :, experts : experts + 1]
    sig = 1.0 / (1.0 + jnp.exp(-hidden))
    silu = hidden * sig
    product = silu * up_value
    part = jnp.sum(product * e, axis=1, keepdims=True)
    grad = scaled * e
    dh = (grad * up_value * (sig * (1.0 + hidden * (1.0 - sig)))).astype(bf16)
    du = (grad * silu).astype(bf16)
    dl = (part * base).astype(bf16)
    pad = jnp.zeros((rows, d_ref.shape[2] - 2 * ff - experts), bf16)
    d_ref[r] = jnp.concatenate([dh, du, dl, pad], axis=1)
    ga_ref[0] = (scaled * product).astype(bf16)

    for q in range(n_group):

        @pl.when(r == q)
        def _():
            d_leaves[q].start()

    @pl.when(i == 1)
    def _():
        copies[1].wait()
        copies[2].wait()
        turned(w_back, w_in_ref[:cols], router_ref[:, :cols])

    @pl.when(i == last)
    def _():
        d = d_ref[...].reshape(n_group * rows, d_ref.shape[2])
        send_back(d, w_back, pa, out_refs, a_sems)
        for c in (x_leaves, *d_leaves):
            c.wait()


def owner_back(slots, far, wide, weights, n_group, pieces, wide_pieces):
    x, gs, h, u, aux = slots
    gate_w, up_w, down_w, router_t, mine = weights
    rows, ff = h.shape[1:]
    width = x.shape[2]
    experts = wide.shape[0]
    n = experts * MAIN
    piece = piece_of(P_SPLIT)

    def turn(i):
        return i + (i == 2).astype(i32) - (i == 3).astype(i32)

    def block(a):
        return pl.BlockSpec((1, *a.shape[1:]), lambda i: (turn(i), 0, 0))

    s = jax.ShapeDtypeStruct
    out = (
        s(x.shape, bf16),
        s((n_group, rows, ff), bf16),
        s((n_group, rows, 2 * ff + 128), bf16),
        *back_shapes(n, P_SPLIT, piece),
    )
    later = (down_w, gate_w, up_w, *far)
    here = pl.BlockSpec(memory_space=pl.ANY)
    return pl.pallas_call(
        functools.partial(back_kernel, n_group, pieces, wide_pieces),
        grid=(n_group,),
        out_shape=out,
        in_specs=[
            block(gs),
            pl.BlockSpec((experts, MAIN, wide.shape[2]), lambda i: (0, turn(i), 0)),
            block(h),
            block(u),
            block(aux),
            whole(router_t),
            whole(mine),
        ]
        + [here] * (len(later) + 1),
        out_specs=[here, block(out[1]), here]
        + [here] * 7,
        scratch_shapes=[
            pltpu.VMEM((1, rows, width), bf16),
            pltpu.VMEM(out[2].shape, bf16),
            pltpu.VMEM((rows, width), bf16),
            pltpu.VMEM((1, rows, ff), f32),
            pltpu.VMEM((1, rows, ff), f32),
            pltpu.VMEM((1, *aux.shape[1:]), f32),
            pltpu.VMEM((1, rows, gs.shape[2]), bf16),
            pltpu.VMEM(down_w.shape, bf16),
            pltpu.VMEM((width, 2 * ff), bf16),
            pltpu.VMEM(far[0].shape, bf16),
            pltpu.VMEM(far[1].shape, bf16),
            pltpu.VMEM((2 * ff + 128, P_SPLIT), bf16),
            pltpu.VMEM((n_group, n, P_SPLIT + piece), bf16),
            pltpu.SemaphoreType.DMA((len(later),)),
            pltpu.SemaphoreType.DMA((P_SPLIT // STEP + 1, 7)),
            pltpu.SemaphoreType.DMA((n_group + 1,)),
        ],
        input_output_aliases={12: 0},
        compiler_params=params(),
        cost_estimate=pl.CostEstimate(
            flops=6 * n_group * rows * width * ff, bytes_accessed=40 * 2**20, transcendentals=n_group * rows * ff
        ),
    )(gs, wide, h, u, aux, router_t, mine, *later, x)


def down_kernel(x_pieces, wide_pieces, gs_ref, wide_ref, ga_ref, far1_ref, far2_ref, out_ref, x, gs, g):
    r = pl.program_id(0)
    first = gs_ref.shape[2]
    n_group, rows, ff = ga_ref.shape
    width = g.shape[2]

    @pl.when(r == 2)
    def _():
        lay_out((far1_ref, far2_ref), width, width + first, x_pieces, x, gs)

    @pl.when(r != 2)
    def _():
        gs[...] = gs_ref[...]

    whole_rows(g.at[r], gs[0], wide_ref, wide_pieces)

    @pl.when(r == n_group - 1)
    def _():
        turned_act = ga_ref[...].reshape(n_group * rows, ff).T
        for c in range(0, width, STEP):
            at = slice(c, c + STEP)
            out_ref[:, at] = dot(turned_act, g[:, :, at].reshape(n_group * rows, STEP)).astype(bf16)


def down_gradient(width, gs, far, wide, g_act, pieces, wide_pieces):
    n_group, rows, ff = g_act.shape
    experts = wide.shape[0]
    out = jax.ShapeDtypeStruct((ff, width), bf16)
    return pl.pallas_call(
        functools.partial(down_kernel, pieces, wide_pieces),
        grid=(n_group,),
        out_shape=out,
        in_specs=[
            pl.BlockSpec((1, *gs.shape[1:]), lambda i: (i, 0, 0)),
            pl.BlockSpec((experts, MAIN, wide.shape[2]), lambda i: (0, i, 0)),
            whole(g_act),
            whole(far[0]),
            whole(far[1]),
        ],
        out_specs=whole(out),
        scratch_shapes=[
            pltpu.VMEM((1, rows, width), bf16),
            pltpu.VMEM((1, rows, gs.shape[2]), bf16),
            pltpu.VMEM((n_group, rows, width), bf16),
        ],
        compiler_params=params(),
        cost_estimate=pl.CostEstimate(
            flops=2 * n_group * rows * width * ff, bytes_accessed=16 * 2**20, transcendentals=0
        ),
    )(gs, wide, g_act, *far)


def x_kernel(experts, x_ref, d_ref, gate_ref, up_ref, router_ref):
    ff = gate_ref.shape[1]
    rows = x_ref.shape[0] * x_ref.shape[1]
    x = x_ref[...].reshape(rows, x_ref.shape[2])
    d = d_ref[...].reshape(rows, d_ref.shape[2])
    both = dot(x.T, d[:, : 2 * ff])
    gate_ref[...] = both[:, :ff].astype(bf16)
    up_ref[...] = both[:, ff:].astype(bf16)
    router_ref[...] = dot(d[:, 2 * ff :], x, ((0,), (0,)))[:experts]


def x_gradients(x_rows, d, ff, experts):
    n_group, rows, width = x_rows.shape
    s = jax.ShapeDtypeStruct
    return pl.pallas_call(
        functools.partial(x_kernel, experts),
        grid=(width // STEP,),
        out_shape=(s((width, ff), bf16), s((width, ff), bf16), s((experts, width), f32)),
        in_specs=[pl.BlockSpec((n_group, rows, STEP), lambda c: (0, 0, c)), whole(d)],
        out_specs=[
            pl.BlockSpec((STEP, ff), lambda c: (c, 0)),
            pl.BlockSpec((STEP, ff), lambda c: (c, 0)),
            pl.BlockSpec((experts, STEP), lambda c: (0, c)),
        ],
        compiler_params=params(),
        cost_estimate=pl.CostEstimate(
            flops=4 * n_group * rows * width * ff, bytes_accessed=12 * 2**20, transcendentals=0
        ),
    )(x_rows, d)


def rest_back_kernel(d_ref, gate_ref, up_ref, router_ref, *refs):
    out_refs = refs[:7]
    w_in, w_back, pa, in_sems, sems = refs[7:]
    n_group, rows = d_ref.shape[:2]
    ff = gate_ref.shape[1]
    cols = w_back.shape[1]
    first = gate_ref.shape[0] - cols
    copies = [
        pltpu.make_async_copy(w.at[pl.ds(first, cols)], w_in.at[:, k * ff : (k + 1) * ff], in_sems.at[k])
        for k, w in enumerate((gate_ref, up_ref))
    ]
    for c in copies:
        c.start()
    for c in copies:
        c.wait()
    turned(w_back, w_in[...], router_ref[:, first:])
    send_back(d_ref[...].reshape(n_group * rows, d_ref.shape[2]), w_back, pa, out_refs, sems)


def rest_back(d, gate_w, up_w, router_t):
    n_group, rows = d.shape[:2]
    width, ff = gate_w.shape
    n = router_t.shape[0] * MAIN
    cols = width - P_SPLIT
    piece = piece_of(cols)
    here = pl.BlockSpec(memory_space=pl.ANY)
    return pl.pallas_call(
        rest_back_kernel,
        out_shape=back_shapes(n, cols, piece),
        in_specs=[pl.BlockSpec(memory_space=pltpu.VMEM), here, here, pl.BlockSpec(memory_space=pltpu.VMEM)],
        out_specs=[here] * 7,
        scratch_shapes=[
            pltpu.VMEM((cols, 2 * ff), bf16),
            pltpu.VMEM((2 * ff + 128, cols), bf16),
            pltpu.VMEM((n_group, n, cols + piece), bf16),
            pltpu.SemaphoreType.DMA((2,)),
            pltpu.SemaphoreType.DMA((cols // STEP + 1, 7)),
        ],
        compiler_params=params(),
        cost_estimate=pl.CostEstimate(
            flops=4 * n_group * rows * ff * cols, bytes_accessed=12 * 2**20, transcendentals=0
        ),
    )(d, gate_w, up_w, router_t)


def finish_kernel(splits, spot_ref, cot_ref, *refs):
    out_ref = refs[-1]
    tok = cot_ref.shape[0]
    spots = spread_spots(spot_ref[...].astype(f32))
    main = put_slot(spots)
    folded = [put_folded(spots, j) for j in range(MAIN // EXTRA)]
    for (first, cols), back_ref in zip(splits, refs[:-1]):
        q = back_ref.shape[1] - cols
        pieces = cols // q
        rows = dot(main, back_ref[:, :cols], ((0,), (0,)))
        more = dot(jnp.concatenate(folded[:pieces], axis=1), back_ref[:, cols:], ((0,), (0,)))
        for j in range(pieces):
            at = slice(j * q, (j + 1) * q)
            to = slice(first + j * q, first + (j + 1) * q)
            total = cot_ref[:, to].astype(f32) + rows[:, at] + more[j * tok : (j + 1) * tok]
            out_ref[:, to] = total.astype(bf16)


def finish(spot, cotang, backs):
    width = cotang.shape[1]
    return pl.pallas_call(
        functools.partial(finish_kernel, ((0, P_SPLIT), (P_SPLIT, width - P_SPLIT))),
        out_shape=jax.ShapeDtypeStruct(cotang.shape, bf16),
        compiler_params=params(SMALL_VMEM),
        cost_estimate=pl.CostEstimate(flops=10**9, bytes_accessed=4 * 2**20, transcendentals=0),
    )(spot, cotang, *backs)


def on_device(saved_inputs, out_cotangent, router, w_gate, w_up, w_down, expert_ids):
    inputs, cotang, router_t = saved_inputs[0], out_cotangent[0], router[0].T
    gate_w, up_w, down_w = w_gate[0, 0], w_up[0, 0], w_down[0, 0]
    experts = lax.axis_size("expert")
    n_group = lax.axis_size("tensor")
    tok, width = inputs.shape
    n_main = experts * MAIN
    pieces = MAIN // EXTRA
    rows = experts * (MAIN + EXTRA)
    ff = gate_w.shape[1]

    send, spot, raw = send_slots(expert_ids[0].T, inputs, cotang, experts, pieces)
    got = exchanged(send.reshape(experts, MAIN, -1)).reshape(n_main, -1)
    wide = wide_slots((raw, *gathered_x(raw)), n_group, experts, pieces)
    got_wide = exchanged(wide)

    mine = (jnp.arange(experts, dtype=i32) == lax.axis_index("expert")).astype(f32)[None, :]
    s = jax.ShapeDtypeStruct
    shapes = (
        s((n_group, rows, width), bf16),
        s((n_group, rows, G_SLOT_COLS), bf16),
        s((n_group, rows, ff), f32),
        s((n_group, rows, ff), f32),
        s((n_group, rows, 2 * experts), f32),
    )
    above_lo, above_hi, far1, far2, below_lo, below_hi = gathered_x(got)
    weights = (gate_w, up_w, router_t, mine)
    slots = slot_rows((got,), weights, shapes, 0, (), pieces)
    slots, above_hi, below_lo = lax.optimization_barrier((slots, above_hi, below_lo))
    slots = slot_rows((above_lo, above_hi), weights, shapes, 1, slots, pieces)
    slots = slot_rows((below_lo, below_hi), weights, shapes, 3, slots, pieces)
    x_rows, g_act, d_all, *part_a = owner_back(
        slots, (far1, far2), got_wide, (gate_w, up_w, down_w, router_t, mine), n_group, pieces, pieces
    )
    part_b = rest_back(d_all, gate_w, up_w, router_t)

    own, far_lo, far_hi, up_lo, up_hi, down_lo, down_hi = part_a
    first_a = ring_first(far_lo, far_hi, up_hi, down_lo)
    x_rows, d_all, first_a = lax.optimization_barrier((x_rows, d_all, first_a))
    grad_gate, grad_up, router_part = x_gradients(x_rows, d_all, ff, experts)
    part_b, router_part = lax.optimization_barrier((part_b, router_part))
    sums_a = ring_second(own, up_lo, down_hi, *first_a)
    back_a = exchanged(sums_a.reshape(experts, MAIN, -1)).reshape(n_main, -1)
    own, far_lo, far_hi, up_lo, up_hi, down_lo, down_hi = part_b
    first_b = ring_first(far_lo, far_hi, up_hi, down_lo)
    router_part, back_a = lax.optimization_barrier((router_part, back_a))
    router_part = ring_total(router_part, along_z)
    g_act, _, _ = lax.optimization_barrier((g_act, first_b, back_a))
    grad_down = down_gradient(width, slots[1], (far1, far2), got_wide, g_act, pieces, pieces)
    sums_b = ring_second(own, up_lo, down_hi, *first_b)
    sums_b, router_part = lax.optimization_barrier((sums_b, router_part))
    back_b = exchanged(sums_b.reshape(experts, MAIN, -1)).reshape(n_main, -1)
    back_b, grad_down = lax.optimization_barrier((back_b, grad_down))
    router_total = ring_total(ring_total(router_part, along_y), along_x)

    cot_out = finish(spot, cotang, (back_a, back_b))
    n_sec = lax.axis_size("section")
    passed = lax.ppermute(cot_out, "section", [((i + 1) % n_sec, i) for i in range(n_sec)])
    return (
        passed[None],
        router_total.T[None],
        grad_gate[None, None],
        grad_up[None, None],
        grad_down[None, None],
    )


def solution(mesh):
    return jax.shard_map(
        on_device,
        mesh=mesh,
        in_specs=(
            P("section", ("expert", "tensor"), None),
            P("section", ("expert", "tensor"), None),
            P("section", None, None),
            P("section", "expert", None, "tensor"),
            P("section", "expert", None, "tensor"),
            P("section", "expert", "tensor", None),
            P("section", ("expert", "tensor"), None),
        ),
        out_specs=(
            P("section", ("expert", "tensor"), None),
            P("section", None, None),
            P("section", "expert", None, "tensor"),
            P("section", "expert", None, "tensor"),
            P("section", "expert", "tensor", None),
        ),
        check_vma=False,
    )
```
